32 devices in a mesh: rep: 8 (over y, x, core), grp: 4 (over z).
Axes of the slice: x: 2, y: 2, z: 4, core: 2. Of those that a mesh axis runs over, the one named last changes fastest.
Arguments:
- tokens: bfloat16 [15360, 1536], P(('rep', 'grp')), may hold values from -6 to 6
- norm_in: bfloat16 [1536], P('grp'), may hold values from 0.5 to 1.5
- in_weight: bfloat16 [1536, 4608], P('grp'), may hold values from -0.15625 to 0.15625
- conv_weight: bfloat16 [1536, 3], P('grp'), may hold values from -3.5 to 3.5
- out_weight: bfloat16 [1536, 1536], P('grp'), may hold values from -0.15625 to 0.15625
- norm_mid: bfloat16 [1536], P('grp'), may hold values from 0.5 to 1.5
- gate_weight: bfloat16 [1536, 6912], P('grp'), may hold values from -0.15625 to 0.15625
- up_weight: bfloat16 [1536, 6912], P('grp'), may hold values from -0.15625 to 0.15625
- down_weight: bfloat16 [6912, 1536], P('grp'), may hold values from -0.15625 to 0.15625
- cotangent: bfloat16 [15360, 1536], P(('rep', 'grp')), may hold values from -6 to 6
Outputs:
- mixed: bfloat16 [15360, 1536], P(('rep', 'grp'))
- input_grad: float32 [15360, 1536], P(('rep', 'grp'))
- norm_in_grad: float32 [1536], P('grp')
- in_weight_grad: float32 [1536, 4608], P('grp')
- conv_weight_grad: float32 [1536, 3], P('grp')
- out_weight_grad: float32 [1536, 1536], P('grp')
- norm_mid_grad: float32 [1536], P('grp')
- gate_weight_grad: float32 [1536, 6912], P('grp')
- up_weight_grad: float32 [1536, 6912], P('grp')
- down_weight_grad: float32 [6912, 1536], P('grp')
The draws below stay inside these ranges and needn't reach their ends.
All inputs are finite; a program needn't handle non-finite values.
Results may differ from the reference program's by a relative error of at most 0.0095.
Values may be sent and summed in bfloat16 or wider, within the bound.
No kernel may reach another device: no remote copies, remote signals or barrier semaphores. Data moves between devices by JAX's collectives and lax.ppermute only.
A program may use at most 512 MiB of HBM per device.

```python
import jax
import jax.numpy as jnp
from jax import lax

D = 1536
FF = 6912
K = 3
TOK_DEV = 480
TOKENS = 15360
N_GRP = 4


def spiked(drawn, stream_key, source, target, parts, factor):
    owner, partner = [(jnp.arange(drawn.shape[dim]) // (drawn.shape[dim] // parts)).reshape([-1 if axis == dim else 1 for axis in range(drawn.ndim)]) for dim in (source, target)]
    chosen = jax.random.permutation(stream_key, parts)[partner]
    strong = (owner == chosen) | (owner == (partner + parts // 2) % parts)
    return jnp.where(strong, factor * drawn, drawn)


def block_scale(own_key, shape, cuts, low, top_value):
    gain, own = 1.0, jax.random.fold_in(own_key, 6)
    for dim, parts in cuts:
        heights = jnp.exp(jax.random.uniform(jax.random.fold_in(own, dim), (parts,), jnp.float32, low / len(cuts), top_value / len(cuts)))
        gain = gain * jnp.repeat(heights, shape[dim] // parts).reshape([-1 if axis == dim else 1 for axis in range(len(shape))])
    return gain


def centred(rng, shape, scale, reach, split=(), held_as=jnp.bfloat16):
    level = block_scale(rng, shape, split, -0.22, 0.18) if split else 1.0
    drawn = jax.random.normal(rng, shape, jnp.float32) * scale * level
    return jnp.minimum(jnp.maximum(drawn, -reach), reach).astype(held_as)


def bell_draw_with(stream_key, extent, deviation, reach, shards, heavy, dtype=jnp.bfloat16):
    drawn = deviation * jax.random.normal(stream_key, extent, jnp.float32)
    if shards:
        drawn = drawn * block_scale(stream_key, extent, shards, -0.22, 0.18)
    return jnp.clip(spiked(drawn, jax.random.fold_in(stream_key, 3), *heavy), -reach, reach).astype(dtype)


def setup_inputs(seed: int = 0) -> dict:
    seeds = jax.random.split(jax.random.key(seed), 11)
    return {
        "tokens": bell_draw_with(seeds[0], (TOKENS, D), 1.0, 6.0, ((0, 32),), (0, 1, 32, 2.75)),
        "norm_in": jnp.clip(1.0 + 0.1 * jax.random.normal(seeds[1], (D,), jnp.float32), 0.5, 1.5).astype(jnp.bfloat16),
        "in_weight": centred(seeds[2], (D, 3 * D), D ** -0.5, 0.15625, ((0, 4),)),
        "conv_weight": centred(seeds[3], (D, K), K ** -0.5, 3.5, ((0, 4),)),
        "out_weight": centred(seeds[4], (D, D), D ** -0.5, 0.15625, ((0, 4),)),
        "norm_mid": jnp.clip(1.0 + 0.1 * jax.random.normal(seeds[5], (D,), jnp.float32), 0.5, 1.5).astype(jnp.bfloat16),
        "gate_weight": centred(seeds[6], (D, FF), D ** -0.5, 0.15625, ((0, 4),)),
        "up_weight": centred(seeds[7], (D, FF), D ** -0.5, 0.15625, ((0, 4),)),
        "down_weight": centred(seeds[8], (FF, D), (FF // 4) ** -0.5, 0.15625, ((0, 4),)),
        "cotangent": bell_draw_with(seeds[9], (TOKENS, D), 1.0, 6.0, ((0, 32),), (0, 1, 32, 2.75)),
    }


EPS = 1e-05

@jax.custom_vjp
def low(v):
    return lax.optimization_barrier(v.astype(jnp.bfloat16)).astype(jnp.float32)

@jax.custom_vjp
def low_back(v):
    return v

def low_keep(v):
    return (low(v), None)

def low_pass(kept, grad):
    return (grad,)

def back_keep(v):
    return (v, None)

def back_low(kept, grad):
    return (low(grad),)
low.defvjp(low_keep, low_pass)
low_back.defvjp(back_keep, back_low)

def matmul(left, right):
    return jnp.dot(left, right, preferred_element_type=jnp.float32, precision=lax.Precision.HIGHEST)

def forward(x, norm_in, in_weight, conv_weight, out_weight, norm_mid, gate_weight, up_weight, down_weight):
    rows = x.shape[0]
    width = x.shape[1]
    taps = conv_weight.shape[1]
    scale_one = lax.rsqrt(lax.optimization_barrier(jnp.mean(x * x, axis=-1, keepdims=True)) + EPS)
    hidden = low(x * scale_one * norm_in)
    bcx = low_back(matmul(hidden, in_weight))
    b_part = bcx[:, :width]
    c_part = bcx[:, width:2 * width]
    x_part = bcx[:, 2 * width:]
    gated = b_part * x_part
    padded = jnp.concatenate([jnp.zeros((taps - 1, width), jnp.float32), gated], axis=0)
    conv = conv_weight[:, 0] * padded[0:rows]
    for tap in range(1, taps):
        conv = conv + conv_weight[:, tap] * padded[tap:tap + rows]
    mixed_in = low(c_part * conv)
    branch = low_back(matmul(mixed_in, out_weight))
    resid = x + branch
    scale_two = lax.rsqrt(lax.optimization_barrier(jnp.mean(resid * resid, axis=-1, keepdims=True)) + EPS)
    second = low(resid * scale_two * norm_mid)
    gate = low_back(matmul(second, gate_weight))
    upper = low_back(matmul(second, up_weight))
    active = low(jax.nn.silu(gate) * upper)
    return resid + matmul(active, down_weight)

def reference(tokens, norm_in, in_weight, conv_weight, out_weight, norm_mid, gate_weight, up_weight, down_weight, cotangent):
    params = tuple((p.astype(jnp.float32) for p in (norm_in, in_weight, conv_weight, out_weight, norm_mid, gate_weight, up_weight, down_weight)))
    seqlen = TOK_DEV * N_GRP
    width = tokens.shape[1]
    inputs = tokens.astype(jnp.float32).reshape(-1, seqlen, width)
    grads_in = cotangent.astype(jnp.float32).reshape(-1, seqlen, width)

    def one_sequence(carry, pair):
        seq_x, seq_g = pair
        result, pull = jax.vjp(forward, seq_x, *params)
        grads = pull(seq_g)
        carry = tuple((c + g for c, g in zip(carry, grads[1:])))
        return (carry, (result.astype(jnp.bfloat16), grads[0]))
    start = tuple((jnp.zeros(p.shape, jnp.float32) for p in params))
    totals, (mixed, input_grad) = lax.scan(one_sequence, start, (inputs, grads_in))
    return (mixed.reshape(-1, width), input_grad.reshape(-1, width), totals[0], totals[1], totals[2], totals[3], totals[4], totals[5], totals[6], totals[7])
```

```python
import jax
import jax.numpy as jnp
from jax import lax
from jax.sharding import PartitionSpec as P

EPS = 1e-05
F32, BF16 = jnp.float32, jnp.bfloat16
CHUNKS = 2


def from_behind(value, axis, steps):
    count = lax.axis_size(axis)
    first, last = (max(0, -steps), min(count, count - steps))
    return lax.ppermute(value, axis, [(source, source + steps) for source in range(first, last)])


def product(left, right):
    return jnp.dot(left, right, preferred_element_type=F32)


def left_product(left, right):
    return lax.dot_general(left, right, (((0,), (0,)), ((), ())), preferred_element_type=F32)


def right_transposed(left, right):
    return lax.dot_general(left, right, (((1,), (1,)), ((), ())), preferred_element_type=F32)


def ring(value):
    count = lax.axis_size("grp")
    return lax.ppermute(value, "grp", [(i, (i + 1) % count) for i in range(count)])


def ring_gather(piece):
    count, me = lax.axis_size("grp"), lax.axis_index("grp")
    out = jnp.zeros((count,) + piece.shape, piece.dtype)
    out = lax.dynamic_update_index_in_dim(out, piece, me, 0)
    for step in range(1, count):
        piece = ring(piece)
        out = lax.dynamic_update_index_in_dim(out, piece, lax.rem(me - step + count, count), 0)
    return out


def ring_scatter(parts):
    count, me = lax.axis_size("grp"), lax.axis_index("grp")
    part = lambda step: lax.dynamic_index_in_dim(
        parts, lax.rem(me - step + 2 * count, count), 0, keepdims=False
    )
    total = part(1)
    for step in range(1, count):
        total = ring(total.astype(BF16)).astype(F32) + part(step + 1).astype(F32)
    return total


def rep_gather(value):
    return lax.all_gather(value, "rep", axis=0, tiled=True)


def rep_scatter(value, axis=0):
    return lax.psum_scatter(value, "rep", scatter_dimension=axis, tiled=True)


def shards(
    tokens,
    norm_in,
    in_weight,
    conv_weight,
    out_weight,
    norm_mid,
    gate_weight,
    up_weight,
    down_weight,
    cotangent,
):
    reps, grps = lax.axis_size("rep"), lax.axis_size("grp")
    rep, grp = lax.axis_index("rep"), lax.axis_index("grp")
    rows, width = tokens.shape
    taps = conv_weight.shape[1]
    own = in_weight.shape[0]
    hidden = gate_weight.shape[1]
    piece = hidden // (reps * grps)
    units = piece * grps
    lanes = -(-units // 128) * 128

    small = jnp.concatenate([norm_in[None], norm_mid[None], conv_weight.T], axis=0)
    small = lax.all_gather(small, "grp", axis=1, tiled=True).astype(F32)
    gain_one, gain_two, taps_f = small[0], small[1], small[2:]
    cut = own // reps
    both = ("grp", "rep")
    w_in = lax.all_gather(
        lax.dynamic_slice_in_dim(in_weight, rep * cut, cut, 0), both, axis=0, tiled=True
    )
    w_out = lax.all_gather(
        lax.dynamic_slice_in_dim(out_weight, rep * cut, cut, 0), both, axis=0, tiled=True
    )

    def columns(weight):
        parts = [
            lax.dynamic_slice(weight, (0, j * (hidden // grps) + rep * piece), (own, piece))
            for j in range(grps)
        ]
        return jnp.concatenate(parts + [jnp.zeros((own, lanes - units), BF16)], axis=1)

    w_pair = ring_gather(jnp.concatenate([columns(gate_weight), columns(up_weight)], axis=1))
    w_pair = w_pair.reshape(width, 2 * lanes)
    w_down = ring_gather(lax.dynamic_slice_in_dim(down_weight, rep * piece, piece, 0))
    w_down = jnp.concatenate(
        [w_down.reshape(units, width), jnp.zeros((lanes - units, width), BF16)], axis=0
    )
    upstream_all = rep_gather(cotangent).reshape(reps, rows, width)

    inputs = tokens.astype(F32)
    scale_one = lax.rsqrt(jnp.mean(inputs * inputs, axis=-1, keepdims=True) + EPS)
    normed = inputs * scale_one
    h_low = (normed * gain_one).astype(BF16)
    bcx = product(h_low, w_in)
    b_part = bcx[:, :width]
    c_part = bcx[:, width : 2 * width]
    x_part = bcx[:, 2 * width :]
    gated = b_part * x_part
    earlier = from_behind(gated[rows - (taps - 1) :], "grp", 1)
    padded = jnp.concatenate([earlier, gated], axis=0)
    conv = taps_f[0] * padded[0:rows]
    for tap in range(1, taps):
        conv = conv + taps_f[tap] * padded[tap : tap + rows]
    z_low = (c_part * conv).astype(BF16)
    resid = inputs + product(z_low, w_out)
    scale_two = lax.rsqrt(jnp.mean(resid * resid, axis=-1, keepdims=True) + EPS)
    normed_two = resid * scale_two
    h2_low = (normed_two * gain_two).astype(BF16)

    part = rows // CHUNKS
    mixed_parts, d_second_parts = [], []
    down_grad, pair_grad = 0.0, 0.0
    for chunk in range(CHUNKS):
        here = slice(chunk * part, (chunk + 1) * part)
        h2 = rep_gather(h2_low[here])
        up_g = upstream_all[:, here].reshape(reps * part, width)
        both_up = product(h2, w_pair)
        gate, upper = both_up[:, :lanes], both_up[:, lanes:]
        sigma = jax.nn.sigmoid(gate)
        swish = gate * sigma
        a_low = (swish * upper).astype(BF16)
        d_active = right_transposed(up_g, w_down)
        d_gate = (d_active * upper * sigma * (1.0 + gate * (1.0 - sigma))).astype(BF16)
        d_upper = (d_active * swish).astype(BF16)
        d_both = jnp.concatenate([d_gate, d_upper], axis=1)
        d_second_parts.append(rep_scatter(right_transposed(d_both, w_pair).astype(BF16)))
        mixed_parts.append(rep_scatter(product(a_low, w_down).astype(BF16)))
        down_grad = down_grad + left_product(a_low, up_g)
        pair_grad = pair_grad + left_product(h2, d_both)
    mixed = (resid + jnp.concatenate(mixed_parts, axis=0).astype(F32)).astype(BF16)
    d_second = jnp.concatenate(d_second_parts, axis=0).astype(F32)

    down_own = ring_scatter(down_grad[:units].astype(BF16).reshape(grps, piece, width))
    pair_own = ring_scatter(pair_grad.astype(BF16).reshape(grps, own, 2 * lanes))
    down_full = rep_gather(down_own.astype(BF16)).astype(F32)
    pair_full = rep_gather(pair_own.astype(BF16)).reshape(reps, own, 2 * lanes)

    def spread(part):
        part = part.reshape(reps, own, grps, piece)
        return part.transpose(1, 2, 0, 3).reshape(own, hidden).astype(F32)

    gate_full = spread(pair_full[:, :, :units])
    up_full = spread(pair_full[:, :, lanes : lanes + units])

    upstream = cotangent.astype(F32)
    local_mid = jnp.sum(d_second * normed_two, axis=0)
    d_normed_two = d_second * gain_two
    d_resid = upstream + scale_two * (
        d_normed_two - normed_two * jnp.mean(d_normed_two * normed_two, axis=-1, keepdims=True)
    )
    d_branch = d_resid.astype(BF16)
    mix_grad = left_product(z_low, d_branch)
    d_z = right_transposed(d_branch, w_out)
    d_c = d_z * conv
    d_conv = d_z * c_part
    later = from_behind(d_conv[: taps - 1], "grp", -1)
    padded_back = jnp.concatenate([d_conv, later], axis=0)
    d_gated = taps_f[0] * padded_back[taps - 1 : taps - 1 + rows]
    for tap in range(1, taps):
        d_gated = d_gated + taps_f[tap] * padded_back[taps - 1 - tap : taps - 1 - tap + rows]
    local_taps = [jnp.sum(d_conv * padded[tap : tap + rows], axis=0) for tap in range(taps)]
    d_bcx = jnp.concatenate([d_gated * x_part, d_c, d_gated * b_part], axis=1).astype(BF16)
    in_grad = left_product(h_low, d_bcx)
    d_hidden = right_transposed(d_bcx, w_in)
    local_in = jnp.sum(d_hidden * normed, axis=0)
    d_normed = d_hidden * gain_one
    input_grad = d_resid + scale_one * (
        d_normed - normed * jnp.mean(d_normed * normed, axis=-1, keepdims=True)
    )

    def whole_sum(grad):
        cols = grad.shape[1]
        grad = rep_scatter(grad.astype(BF16).reshape(grps, reps, cut, cols), axis=1)
        return rep_gather(ring_scatter(grad.reshape(grps, cut, cols)).astype(BF16)).astype(F32)

    out_full = whole_sum(mix_grad)
    in_full = whole_sum(in_grad)
    sums = lax.psum(jnp.stack([local_in, local_mid] + local_taps), ("rep", "grp"))
    sums = lax.dynamic_slice_in_dim(sums, grp * own, own, 1)
    return (
        mixed,
        input_grad,
        sums[0],
        in_full,
        sums[2:].T,
        out_full,
        sums[1],
        gate_full,
        up_full,
        down_full,
    )


def solution(mesh):
    placed = (
        P(("rep", "grp"), None),
        P("grp"),
        P("grp", None),
        P("grp", None),
        P("grp", None),
        P("grp"),
        P("grp", None),
        P("grp", None),
        P("grp", None),
        P(("rep", "grp"), None),
    )
    return jax.shard_map(
        shards,
        mesh=mesh,
        in_specs=placed,
        out_specs=(
            P(("rep", "grp"), None),
            P(("rep", "grp"), None),
            P("grp"),
            P("grp", None),
            P("grp", None),
            P("grp", None),
            P("grp"),
            P("grp", None),
            P("grp", None),
            P("grp", None),
        ),
        check_vma=False,
    )
```

```python
import functools

import jax
import jax.numpy as jnp
from jax import lax
from jax.experimental import pallas as pl
from jax.experimental.pallas import tpu as pltpu
from jax.sharding import PartitionSpec as P

EPS = 1e-05
F32, BF16 = jnp.float32, jnp.bfloat16
LIGHT = pl.CostEstimate(flops=1, bytes_accessed=1, transcendentals=0)


def after(value, *others):
    return lax.optimization_barrier((value,) + others)[0]


def from_behind(value, axis, steps):
    count = lax.axis_size(axis)
    first, last = (max(0, -steps), min(count, count - steps))
    return lax.ppermute(value, axis, [(source, source + steps) for source in range(first, last)])


def product(left, right):
    return jnp.dot(left, right, preferred_element_type=F32)


def left_product(left, right):
    return lax.dot_general(left, right, (((0,), (0,)), ((), ())), preferred_element_type=F32)


def right_transposed(left, right):
    return lax.dot_general(left, right, (((1,), (1,)), ((), ())), preferred_element_type=F32)


def turn(value, places):
    count = lax.axis_size("grp")
    return lax.ppermute(value, "grp", [(i, (i + places) % count) for i in range(count)])


def behind(places):
    count = lax.axis_size("grp")
    return lax.rem(lax.axis_index("grp") - places + count, count)


def placed(values):
    out = jnp.zeros((len(values),) + values[0].shape, values[0].dtype)
    for places, value in enumerate(values):
        out = lax.dynamic_update_index_in_dim(out, value, behind(places), 0)
    return out


def sends(parts):
    return [
        lax.dynamic_index_in_dim(parts, behind(-places), 0, keepdims=False)
        for places in range(lax.axis_size("grp"))
    ]


def turned(parts):
    return parts[:1] + [turn(part, places + 1) for places, part in enumerate(parts[1:])]


def total(parts):
    return sum(part.astype(F32) for part in parts)


def flip(value, bit):
    return lax.ppermute(value, "rep", [(i, i ^ bit) for i in range(lax.axis_size("rep"))])


def pair(mine, other, bit, axis):
    low = (lax.axis_index("rep") & bit) == 0
    return jnp.stack([jnp.where(low, mine, other), jnp.where(low, other, mine)], axis)


def same_core():
    chips = lax.axis_size("rep") // 2
    return [[2 * chip + core for chip in range(chips)] for core in range(2)]


def chips_gather(value):
    return lax.all_gather(value, "rep", axis=0, axis_index_groups=same_core())


def chips_gather_two(one, two):
    if lax.axis_size("rep") != 8:
        return chips_gather(one), chips_gather(two)
    one_x, two_y = flip(one, 2), flip(two, 4)
    one, two = pair(one, one_x, 2, 0), pair(two, two_y, 4, 0)
    one_y, two_x = flip(one, 4), flip(two, 2)
    one, two = pair(one, one_y, 4, 0), pair(two, two_x, 2, 1)
    return one.reshape((4,) + one.shape[2:]), two.reshape((4,) + two.shape[2:])


def chips_gather_steps(value):
    half = value.shape[-1] // 2
    return jnp.concatenate(chips_gather_two(value[..., :half], value[..., half:]), axis=-1)


def chips_scatter(value):
    return lax.psum_scatter(
        value, "rep", scatter_dimension=0, tiled=True, axis_index_groups=same_core()
    )


def chips_scatter_steps(value):
    if lax.axis_size("rep") != 8:
        return chips_scatter(value).astype(F32)
    rep = lax.axis_index("rep")
    rows, half = value.shape[0] // 4, value.shape[1] // 2

    def split(part, bit, axis):
        mine = jnp.where((rep & bit) == 0, 0, 1)
        pick = lambda i: lax.dynamic_index_in_dim(part, i, axis, keepdims=False)
        return pick(mine).astype(F32), pick(1 - mine).astype(BF16)

    value = value.reshape(2, 2, rows, 2 * half)
    one, send_one = split(value[..., :half], 2, 1)
    two, send_two = split(value[..., half:], 4, 0)
    one, two = one + flip(send_one, 2).astype(F32), two + flip(send_two, 4).astype(F32)
    one, send_one = split(one, 4, 0)
    two, send_two = split(two, 2, 0)
    one, two = one + flip(send_one, 4).astype(F32), two + flip(send_two, 2).astype(F32)
    return jnp.concatenate([one, two], axis=-1)


def rep_scatter(value):
    return lax.psum_scatter(value, "rep", scatter_dimension=0, tiled=True)


def rep_gather(value):
    return lax.all_gather(value, "rep", axis=0)


def spread_kernel(piece, groups, pair_ref, gate_ref, up_ref):
    reps, _, lanes = pair_ref.shape
    for start, out_ref in ((0, gate_ref), (lanes // 2, up_ref)):
        for j in range(groups):
            for rep in range(reps):
                place = (j * reps + rep) * piece
                out_ref[:, place : place + piece] = pair_ref[
                    rep, :, start + j * piece : start + (j + 1) * piece
                ].astype(F32)


def spread(part, groups, piece):
    reps, rows, lanes = part.shape
    hidden = reps * groups * piece
    tile = 64
    return pl.pallas_call(
        functools.partial(spread_kernel, piece, groups),
        grid=(rows // tile,),
        in_specs=[pl.BlockSpec((reps, tile, lanes), lambda i: (0, i, 0))],
        out_specs=[pl.BlockSpec((tile, hidden), lambda i: (i, 0))] * 2,
        out_shape=[jax.ShapeDtypeStruct((rows, hidden), F32)] * 2,
        compiler_params=pltpu.CompilerParams(vmem_limit_bytes=60 * 2**20),
        cost_estimate=pl.CostEstimate(flops=0, bytes_accessed=rows * hidden * 12, transcendentals=0),
    )(part)


def place_kernel(count, steps, table_ref, *refs):
    del table_ref
    step = pl.program_id(0)
    left_ref, right_ref = refs[-2:]
    for k in range(count):

        @pl.when((step >= k * steps) & (step < (k + 1) * steps))
        def _(k=k):
            left_ref[...] = refs[2 * k][0, 0]
            right_ref[...] = refs[2 * k + 1][0, 0]


def place_weights(left, right, pieces, cores, near, rep, grp):
    _, turns, cut, cols = pieces[0].shape
    own = left.shape[0] // (turns + 1)
    x, y = (rep >> 1) & 1, rep >> 2
    if not near:
        x, y = 1 - x, 1 - y
    rows = lambda places, chip, core: behind(places) * (own // cut) + 2 * chip + core
    table = jnp.stack(
        [
            rows(places, chip, core)
            for which in range(2)
            for core in cores
            for line in range(2)
            for places in range(1, turns + 1)
            for chip in ((2 * y + line, 2 * line + x)[which],)
        ]
    )
    count, steps = len(cores), 2 * turns

    def came(k):
        def index(i, table):
            step = jnp.clip(i - k * steps, 0, steps - 1)
            return (step // turns, step % turns, 0, 0)

        return pl.BlockSpec((1, 1, cut, cols), index)

    anywhere = pl.BlockSpec(memory_space=pl.ANY)
    total_steps = count * steps
    return pl.pallas_call(
        lambda table_ref, *refs: place_kernel(count, steps, table_ref, *refs[2:]),
        grid_spec=pltpu.PrefetchScalarGridSpec(
            num_scalar_prefetch=1,
            grid=(total_steps,),
            in_specs=[anywhere] * 2 + [came(k // 2) for k in range(2 * count)],
            out_specs=[
                pl.BlockSpec((cut, cols), lambda i, table: (table[i], 0)),
                pl.BlockSpec((cut, cols), lambda i, table: (table[total_steps + i], 0)),
            ],
        ),
        out_shape=[jax.ShapeDtypeStruct(left.shape, BF16)] * 2,
        input_output_aliases={1: 0, 2: 1},
        compiler_params=pltpu.CompilerParams(vmem_limit_bytes=60 * 2**20),
        cost_estimate=LIGHT,
    )(table, left, right, *pieces)


def in_kernel(tokens_ref, gain_ref, b_ref, c_ref, x_ref, h_ref, scale_ref, b_out, c_out, x_out, edge_ref):
    @pl.when(pl.program_id(0) == 0)
    def _():
        inputs = tokens_ref[...].astype(F32)
        scale = lax.rsqrt(jnp.mean(inputs * inputs, axis=-1, keepdims=True) + EPS)
        scale_ref[...] = scale
        h_ref[...] = (inputs * scale * gain_ref[...]).astype(BF16)

    h_low = h_ref[...]
    b_part = product(h_low, b_ref[...])
    x_part = product(h_low, x_ref[...])
    b_out[...] = b_part
    x_out[...] = x_part
    c_out[...] = product(h_low, c_ref[...])
    edge_ref[...] = (b_part * x_part)[-edge_ref.shape[0] :]


def in_forward(tokens, gain, left, right):
    rows, width = tokens.shape
    cols = 256
    count = width // cols
    whole = pl.BlockSpec((rows, width), lambda i: (0, 0))
    column = pl.BlockSpec((rows, cols), lambda i: (0, i))
    weight = lambda start: pl.BlockSpec((width, cols), lambda i: (0, start + i))
    part = jax.ShapeDtypeStruct((rows, width), F32)
    return pl.pallas_call(
        in_kernel,
        grid=(count,),
        in_specs=[
            whole,
            pl.BlockSpec((1, width), lambda i: (0, 0)),
            weight(0),
            weight(count),
            weight(0),
        ],
        out_specs=[
            whole,
            pl.BlockSpec((rows, 1), lambda i: (0, 0)),
            column,
            column,
            column,
            pl.BlockSpec((8, cols), lambda i: (0, i)),
        ],
        out_shape=[
            jax.ShapeDtypeStruct((rows, width), BF16),
            jax.ShapeDtypeStruct((rows, 1), F32),
            part,
            part,
            part,
            jax.ShapeDtypeStruct((8, width), F32),
        ],
        compiler_params=pltpu.CompilerParams(vmem_limit_bytes=60 * 2**20),
        cost_estimate=LIGHT,
    )(tokens, gain, left, left, right)


def out_kernel(
    tokens_ref, gain_ref, taps_ref, earlier_ref, b_ref, c_ref, x_ref, w_ref,
    gated_ref, conv_ref, z_ref, resid_ref, normed_ref, scale_ref, h2_ref, sum_ref,
):
    step = pl.program_id(0)
    rows = b_ref.shape[0]
    gated = b_ref[...] * x_ref[...]
    gated_ref[...] = gated
    padded = jnp.concatenate([earlier_ref[...], gated], axis=0)
    conv = taps_ref[0:1] * padded[0:rows]
    for tap in range(1, taps_ref.shape[0]):
        conv = conv + taps_ref[tap : tap + 1] * padded[tap : tap + rows]
    conv_ref[...] = conv
    z_low = (c_ref[...] * conv).astype(BF16)
    z_ref[...] = z_low

    @pl.when(step == 0)
    def _():
        sum_ref[...] = tokens_ref[...].astype(F32)

    sum_ref[...] += product(z_low, w_ref[...])

    @pl.when(step == pl.num_programs(0) - 1)
    def _():
        resid = sum_ref[...]
        resid_ref[...] = resid
        scale = lax.rsqrt(jnp.mean(resid * resid, axis=-1, keepdims=True) + EPS)
        scale_ref[...] = scale
        normed = resid * scale
        normed_ref[...] = normed
        h2_ref[...] = (normed * gain_ref[...]).astype(BF16)


def out_forward(tokens, gain, taps_f, earlier, b_part, c_part, x_part, right):
    rows, width = tokens.shape
    cols = 256
    whole = pl.BlockSpec((rows, width), lambda i: (0, 0))
    column = lambda n: pl.BlockSpec((n, cols), lambda i: (0, i))
    full = lambda kind: jax.ShapeDtypeStruct((rows, width), kind)
    return pl.pallas_call(
        out_kernel,
        grid=(width // cols,),
        in_specs=[
            whole,
            pl.BlockSpec((1, width), lambda i: (0, 0)),
            column(taps_f.shape[0]),
            column(earlier.shape[0]),
            column(rows),
            column(rows),
            column(rows),
            pl.BlockSpec((cols, width), lambda i: (i, 1)),
        ],
        out_specs=[
            column(rows),
            column(rows),
            column(rows),
            whole,
            whole,
            pl.BlockSpec((rows, 1), lambda i: (0, 0)),
            whole,
        ],
        out_shape=[
            full(F32),
            full(F32),
            full(BF16),
            full(F32),
            full(F32),
            jax.ShapeDtypeStruct((rows, 1), F32),
            full(BF16),
        ],
        scratch_shapes=[pltpu.VMEM((rows, width), F32)],
        compiler_params=pltpu.CompilerParams(vmem_limit_bytes=60 * 2**20),
        cost_estimate=LIGHT,
    )(tokens, gain, taps_f, earlier, b_part, c_part, x_part, right)


def mid_kernel(
    second0_ref, second1_ref, up_ref, normed_ref, scale_ref, gain_ref, w_ref, conv_ref, c_ref,
    resid_ref, branch_ref, d_c_ref, d_conv_ref, sum_ref,
):
    step, half_steps = pl.program_id(0), pl.num_programs(0) // 2

    @pl.when(step == 0)
    def _():
        sum_ref[...] = jnp.zeros_like(sum_ref)

    d_second = jnp.where(step < half_steps, second0_ref[...], second1_ref[...]).astype(F32)
    normed = normed_ref[...]
    both = d_second * normed
    sum_ref[...] += jnp.sum(both, axis=0, keepdims=True)
    d_normed = d_second * gain_ref[...]
    mean = jnp.mean(d_normed * normed, axis=-1, keepdims=True)
    d_resid = up_ref[...].astype(F32) + scale_ref[...] * (d_normed - normed * mean)
    resid_ref[...] = d_resid
    branch = d_resid.astype(BF16)
    branch_ref[...] = branch
    d_z = right_transposed(branch, w_ref[...])
    d_c_ref[...] = (d_z * conv_ref[...]).astype(BF16)
    d_conv_ref[...] = d_z * c_ref[...]


def mid_backward(second0, second1, upstream, normed, scale, gain, right, conv, c_part):
    rows, width = normed.shape
    tile = rows // 2
    steps = 2
    row = pl.BlockSpec((tile, width), lambda i: (i, 0))
    first = pl.BlockSpec((tile, width), lambda i: (jnp.minimum(i, steps // 2 - 1), 0))
    last = pl.BlockSpec((tile, width), lambda i: (jnp.maximum(i - steps // 2, 0), 0))
    line = pl.BlockSpec((1, width), lambda i: (0, 0))
    return pl.pallas_call(
        mid_kernel,
        grid=(steps,),
        in_specs=[
            first,
            last,
            row,
            row,
            pl.BlockSpec((tile, 1), lambda i: (i, 0)),
            line,
            pl.BlockSpec((width, width), lambda i: (0, 1)),
            row,
            row,
        ],
        out_specs=[row, row, row, row, line],
        out_shape=[
            jax.ShapeDtypeStruct((rows, width), F32),
            jax.ShapeDtypeStruct((rows, width), BF16),
            jax.ShapeDtypeStruct((rows, width), BF16),
            jax.ShapeDtypeStruct((rows, width), F32),
            jax.ShapeDtypeStruct((1, width), F32),
        ],
        compiler_params=pltpu.CompilerParams(vmem_limit_bytes=60 * 2**20),
        cost_estimate=LIGHT,
    )(second0, second1, upstream, normed, scale, gain, right, conv, c_part)


def taps_kernel(d_conv_ref, later_ref, taps_ref, b_ref, x_ref, u_ref, earlier_ref, d_c_ref, branch_ref, all_ref, sum_ref):
    rows = d_conv_ref.shape[0]
    taps = taps_ref.shape[0]
    d_conv = d_conv_ref[...]
    after_it = jnp.concatenate([d_conv, later_ref[...]], axis=0)
    before_it = jnp.concatenate([earlier_ref[...], u_ref[...]], axis=0)
    d_gated = jnp.zeros_like(d_conv)
    for tap in range(taps):
        ahead = taps - 1 - tap
        d_gated = d_gated + taps_ref[tap : tap + 1] * after_it[ahead : ahead + rows]
        sum_ref[tap : tap + 1] = jnp.sum(d_conv * before_it[tap : tap + rows], axis=0, keepdims=True)
    all_ref[0, 0] = (d_gated * x_ref[...]).astype(BF16)
    all_ref[1, 0] = d_c_ref[...]
    all_ref[2, 0] = (d_gated * b_ref[...]).astype(BF16)
    all_ref[3, 0] = branch_ref[...]


def taps_backward(d_conv, later, taps_f, b_part, x_part, gated, earlier, d_c, branch, block):
    rows, width = d_conv.shape
    taps = taps_f.shape[0]
    cols = 256
    per = block // cols
    column = lambda n: pl.BlockSpec((n, cols), lambda i: (0, i))
    d_all, sums = pl.pallas_call(
        taps_kernel,
        grid=(width // cols,),
        in_specs=[
            column(rows),
            column(taps - 1),
            column(taps),
            column(rows),
            column(rows),
            column(rows),
            column(taps - 1),
            column(rows),
            column(rows),
        ],
        out_specs=[
            pl.BlockSpec((4, 1, rows, cols), lambda i: (0, i // per, 0, i % per)),
            column(taps),
        ],
        out_shape=[
            jax.ShapeDtypeStruct((4, width // block, rows, block), BF16),
            jax.ShapeDtypeStruct((taps, width), F32),
        ],
        compiler_params=pltpu.CompilerParams(vmem_limit_bytes=60 * 2**20),
        cost_estimate=LIGHT,
    )(d_conv, later, taps_f, b_part, x_part, gated, earlier, d_c, branch)
    return d_all.reshape(-1, rows, block), sums


def ffn_kernel(count, core_ref, *refs):
    del core_ref
    h2_refs, (up_ref, pair_ref, down_ref, act_ref, both_ref, second_ref, mixed_ref) = (
        refs[:count],
        refs[count:],
    )
    lanes = down_ref.shape[0]
    h2 = h2_refs[0][...]
    if count == 2:
        h2 = jnp.where(pl.program_id(0) < pl.num_programs(0) // 2, h2, h2_refs[1][...])
    both = product(h2, pair_ref[...])
    gate, upper = both[:, :lanes], both[:, lanes:]
    sigma = jax.nn.sigmoid(gate)
    swish = gate * sigma
    act = (swish * upper).astype(BF16)
    act_ref[...] = act
    d_act = right_transposed(up_ref[...], down_ref[...])
    both_ref[:, :lanes] = (d_act * upper * sigma * (1.0 + gate * (1.0 - sigma))).astype(BF16)
    both_ref[:, lanes:] = (d_act * swish).astype(BF16)
    second_ref[...] = right_transposed(both_ref[...], pair_ref[...]).astype(BF16)
    mixed_ref[...] = product(act, down_ref[...]).astype(BF16)


def ffn(h2s, up_g, w_pair, w_down, core, reps):
    tokens, width = up_g.shape
    lanes = w_down.shape[0]
    chips = reps // 2
    tile = tokens // reps
    if len(h2s) == 2:
        ordered = lambda i, core: (
            2 * (i % chips) + jnp.where(i < chips, core[0], 1 - core[0]),
            0,
        )
        firsts = [
            lambda i, core: (jnp.minimum(i, chips - 1), 0),
            lambda i, core: (jnp.maximum(i - chips, 0), 0),
        ]
    else:
        tile *= 2
        ordered = lambda i, core: (i, 0)
        firsts = [ordered]
    plain = lambda i, core: (i, 0)
    spec = lambda n, index: pl.BlockSpec((tile, n), index)
    full = lambda w: pl.BlockSpec(w.shape, lambda i, core: (0, 0), pipeline_mode=pl.Buffered(1))
    return pl.pallas_call(
        functools.partial(ffn_kernel, len(h2s)),
        grid_spec=pltpu.PrefetchScalarGridSpec(
            num_scalar_prefetch=1,
            grid=(tokens // tile,),
            in_specs=[spec(width, index) for index in firsts]
            + [spec(width, ordered), full(w_pair), full(w_down)],
            out_specs=[
                spec(lanes, ordered),
                spec(2 * lanes, plain),
                spec(width, ordered),
                spec(width, ordered),
            ],
        ),
        out_shape=[
            jax.ShapeDtypeStruct((tokens, n), BF16) for n in (lanes, 2 * lanes, width, width)
        ],
        compiler_params=pltpu.CompilerParams(vmem_limit_bytes=60 * 2**20),
        cost_estimate=pl.CostEstimate(flops=17 * tokens * width * lanes, bytes_accessed=0, transcendentals=0),
    )(core, *h2s, up_g, w_pair, w_down)


def grad_kernel(parts, lefts_count, *refs):
    lefts, rights, out_ref, total_ref = (
        refs[:lefts_count],
        refs[lefts_count:-2],
        refs[-2],
        refs[-1],
    )
    step = pl.program_id(0)

    @pl.when(step == 0)
    def _():
        total_ref[...] = jnp.zeros_like(total_ref)

    for start, stop, left, right in parts:

        @pl.when((step >= start) & (step < stop))
        def _(left=left, right=right):
            total_ref[...] += left_product(lefts[left][...], rights[right][...])

    @pl.when(step == pl.num_programs(0) - 1)
    def _():
        out_ref[...] = total_ref[...].astype(BF16)


def grad(lefts, rights, columns=None, place=0):
    tile = 480
    n, m = lefts[0].shape[1], columns or rights[0].shape[1]

    def cuts(arrays):
        out = [0]
        for array in arrays:
            out.append(out[-1] + array.shape[0] // tile)
        return out

    left_cuts, right_cuts = cuts(lefts), cuts(rights)
    edges = sorted(set(left_cuts + right_cuts))
    find = lambda which, step: max(k for k in range(len(which) - 1) if which[k] <= step)
    parts = [
        (start, stop, find(left_cuts, start), find(right_cuts, start))
        for start, stop in zip(edges, edges[1:])
    ]

    def spec(which, k, cols, place):
        low, high = which[k], which[k + 1]
        return pl.BlockSpec((tile, cols), lambda i: (jnp.clip(i, low, high - 1) - low, place))

    return pl.pallas_call(
        functools.partial(grad_kernel, parts, len(lefts)),
        grid=(edges[-1],),
        in_specs=[spec(left_cuts, k, n, 0) for k in range(len(lefts))]
        + [spec(right_cuts, k, m, place) for k in range(len(rights))],
        out_specs=pl.BlockSpec((n, m), lambda i: (0, 0)),
        out_shape=jax.ShapeDtypeStruct((n, m), BF16),
        scratch_shapes=[pltpu.VMEM((n, m), F32)],
        compiler_params=pltpu.CompilerParams(vmem_limit_bytes=60 * 2**20),
        cost_estimate=pl.CostEstimate(flops=3 * tile * edges[-1] * n * m, bytes_accessed=0, transcendentals=0),
    )(*lefts, *rights)


def block_kernel(count, kept, places_ref, *refs):
    del places_ref
    lefts, rights, refs = refs[:count], refs[count : 2 * count], refs[2 * count :]
    for k in range(count):
        total_ = left_product(lefts[k][0], rights[k][0])
        if not kept:
            refs[k][...] = total_.astype(BF16)
            continue
        total_ = total_ + refs[k][...].astype(F32)
        for which in range(2):

            @pl.when(pl.program_id(0) == which)
            def _(k=k, which=which, total_=total_):
                ref = refs[count + 2 * k + which]
                ref[...] = total_.astype(ref.dtype)


def block_grads(places, lefts, rights, came=(), kept=()):
    count = places.shape[0]
    rows, width = lefts.shape[1:]
    blocks, _, block = rights.shape
    branch = blocks - blocks // 4
    left = lambda k: pl.BlockSpec(
        (1, rows, width // 2), lambda i, places: ((places[k] >= branch).astype(jnp.int32), 0, i)
    )
    right = lambda k: pl.BlockSpec((1, rows, block), lambda i, places: (places[k], 0, 0))
    moving = pl.BlockSpec((width // 2, block), lambda i, places: (i, 0))
    fixed = pl.BlockSpec((width // 2, block), lambda i, places: (0, 0))
    if kept:
        outs = [jax.ShapeDtypeStruct((width // 2, block), kind) for kind in kept]
    else:
        outs = [jax.ShapeDtypeStruct((width, block), BF16)] * count
    return pl.pallas_call(
        functools.partial(block_kernel, count, bool(kept)),
        grid_spec=pltpu.PrefetchScalarGridSpec(
            num_scalar_prefetch=1,
            grid=(2,),
            in_specs=[left(k) for k in range(count)]
            + [right(k) for k in range(count)]
            + [moving for _ in came],
            out_specs=[fixed if kept else moving for _ in outs],
        ),
        out_shape=outs,
        compiler_params=pltpu.CompilerParams(vmem_limit_bytes=40 * 2**20),
        cost_estimate=LIGHT,
    )(places, *([lefts] * count), *([rights] * count), *came)


def unblock_kernel(core_ref, same_ref, other_ref, in_ref, out_ref):
    chips, _, block = same_ref.shape
    first = core_ref[0] == 0
    for chip in range(chips):
        same, other = same_ref[chip].astype(F32), other_ref[chip].astype(F32)
        for core, value in enumerate((jnp.where(first, same, other), jnp.where(first, other, same))):
            place = (2 * chip + core) * block
            if place < in_ref.shape[1]:
                in_ref[:, place : place + block] = value
            else:
                place -= in_ref.shape[1]
                out_ref[:, place : place + block] = value


def unblock(core, same, other, width):
    chips, rows, block = same.shape
    tile = 96
    spec = pl.BlockSpec((chips, tile, block), lambda i, core: (0, i, 0))
    return pl.pallas_call(
        unblock_kernel,
        grid_spec=pltpu.PrefetchScalarGridSpec(
            num_scalar_prefetch=1,
            grid=(rows // tile,),
            in_specs=[spec, spec],
            out_specs=[pl.BlockSpec((tile, n), lambda i, core: (i, 0)) for n in (3 * width, width)],
        ),
        out_shape=[jax.ShapeDtypeStruct((rows, n), F32) for n in (3 * width, width)],
        compiler_params=pltpu.CompilerParams(vmem_limit_bytes=60 * 2**20),
        cost_estimate=pl.CostEstimate(flops=0, bytes_accessed=24 * rows * width, transcendentals=0),
    )(core, same, other)


def shards(
    tokens,
    norm_in,
    in_weight,
    conv_weight,
    out_weight,
    norm_mid,
    gate_weight,
    up_weight,
    down_weight,
    cotangent,
):
    reps, grps = lax.axis_size("rep"), lax.axis_size("grp")
    rep, grp = lax.axis_index("rep"), lax.axis_index("grp")
    chips = reps // 2
    low_core = (rep & 1) == 0
    rows, width = tokens.shape
    taps = conv_weight.shape[1]
    own = in_weight.shape[0]
    hidden = gate_weight.shape[1]
    piece = hidden // (reps * grps)
    units = piece * grps
    lanes = -(-units // 128) * 128
    half = rows // 2

    def columns(weight):
        parts = [
            lax.dynamic_slice(weight, (0, j * (hidden // grps) + rep * piece), (own, piece))
            for j in range(grps)
        ]
        return jnp.concatenate(parts + [jnp.zeros((own, lanes - units), BF16)], axis=1)

    pair_piece = jnp.concatenate([columns(gate_weight), columns(up_weight)], axis=1)
    down_piece = lax.dynamic_slice_in_dim(down_weight, rep * piece, piece, 0)
    cut = own // reps
    gains = jnp.concatenate([norm_in[None], norm_mid[None], conv_weight.T], axis=0)
    sent = jnp.concatenate(
        [
            lax.dynamic_slice_in_dim(in_weight, rep * cut, cut, 0),
            lax.dynamic_slice_in_dim(out_weight, rep * cut, cut, 0),
        ],
        axis=1,
    )
    fast = reps == 8 and grps == 4
    if fast:
        def first(value):
            half_cols = value.shape[-1] // 2
            return [value[..., :half_cols], value[..., half_cols:]]

        def swap(values, bits):
            return [flip(value, bit) for value, bit in zip(values, bits)]

        def second(values, came):
            return [pair(values[0], came[0], 2, 0), pair(values[1], came[1], 4, 0)]

        def third(values, came):
            both = [pair(values[0], came[0], 4, 0), pair(values[1], came[1], 2, 1)]
            return jnp.concatenate([value.reshape((4,) + value.shape[2:]) for value in both], axis=-1)

        side = -(-gains.size // (cut * 128)) * 128
        gains = jnp.pad(gains.reshape(-1), (0, cut * side - gains.size)).reshape(cut, side)
        sent = jnp.concatenate([sent, gains], axis=1)
        near = [turn(sent, 1), turn(sent, 3)]
        ups = first(cotangent)
        left = jnp.zeros((width, 2 * width), BF16)
        left = lax.dynamic_update_slice(left, in_weight[:, : 2 * width], (grp * own, 0))
        right = jnp.zeros((width, 2 * width), BF16)
        right = lax.dynamic_update_slice(right, in_weight[:, 2 * width :], (grp * own, 0))
        right = lax.dynamic_update_slice(right, out_weight, (grp * own, width))
        came = [after(value, pair_piece, left, right, *near) for value in swap(ups, (2, 4))]
        ups = second(ups, came)
        far = turn(after(sent, *near), 2)
        w_pair = lax.all_gather(after(pair_piece, *near), "grp", axis=0, tiled=True)
        came = swap(ups, (4, 2))
        hops = [near[0], far, near[1]]
        small = placed([gains] + [value[:, 4 * width :] for value in hops])
        small = small.reshape(grps, -1)[:, : (2 + taps) * own].reshape(grps, 2 + taps, own)
        turns = first(jnp.stack([value[:, : 4 * width] for value in hops]))
        turns_came = swap(turns, (2, 4))
        ups = third(ups, [after(value, *turns) for value in came])
        ups_other = flip(ups, 1)
        up_halves = [
            pair(ups[:, rows_of], ups_other[:, rows_of], 1, 1).reshape(reps * half, width)
            for rows_of in (slice(0, half), slice(half, rows))
        ]
        turns_came = [after(value, *up_halves) for value in turns_came]
        pieces = second(turns, turns_came)
        cores = (rep & 1, 1 - (rep & 1))
        came = swap(pieces, (4, 2))
        pieces += [flip(value, 1) for value in pieces]
        left, right = place_weights(left, right, pieces, cores, True, rep, grp)
        pieces = [after(value, left) for value in came]
        pieces += [flip(value, 1) for value in pieces]
        left, right = place_weights(left, right, pieces, cores, False, rep, grp)
        w_down = lax.all_gather(after(down_piece, pair_piece), "grp", axis=0, tiled=True)
    else:
        w_pair = lax.all_gather(pair_piece, "grp", axis=0, tiled=True)
        w_down = lax.all_gather(down_piece, "grp", axis=0, tiled=True)
        whole = lax.all_gather(sent, ("grp", "rep"), axis=0, tiled=True)
        left, right = whole[:, : 2 * width], whole[:, 2 * width :]
        small = lax.all_gather(gains, "grp", axis=0)
        upstream_all = rep_gather(cotangent)
        up_halves = [
            upstream_all[:, rows_of].reshape(reps * half, width)
            for rows_of in (slice(0, half), slice(half, rows))
        ]
    small = small.swapaxes(0, 1).reshape(2 + taps, width).astype(F32)
    gain_one, gain_two, taps_f = small[0], small[1], small[2:]

    h_low, scale_one, b_part, c_part, x_part, edge = in_forward(tokens, gain_one[None], left, right)
    earlier = from_behind(edge[edge.shape[0] - (taps - 1) :], "grp", 1)
    gated, conv, z_low, resid, normed_two, scale_two, h2_low = out_forward(
        tokens,
        gain_two[None],
        taps_f,
        earlier,
        b_part,
        c_part,
        x_part,
        right,
    )
    w_x, w_out = right[:, :width], right[:, width:]

    flat = lambda value: value.reshape(reps * half, width)
    flat_half = lambda value: value.reshape(chips * half, width)
    if fast:
        parts = first(h2_low[:half])
        came = swap(parts, (2, 4))
        parts = second(parts, [after(value, w_pair) for value in came])
        came = swap(parts, (4, 2))
        same = flat_half(third(parts, [after(value, w_down) for value in came]))
        h2s = [same, flip(same, 1)]
    else:
        h2s = [flat(rep_gather(h2_low[:half]))]
    h2_last = h2_low[half:]
    if fast:
        h2_last = after(h2_last, *came)
    h2_last = flat(rep_gather(h2_last))
    w_down = jnp.concatenate([w_down, jnp.zeros((lanes - units, width), BF16)], axis=0)
    ups = up_halves

    core = (rep & 1).reshape(1)
    acts, boths, second0, mixed0 = ffn(h2s, ups[0], w_pair, w_down, core, reps)
    acts1, boths1, second1, mixed1 = ffn(
        [after(h2_last, second0)], ups[1], w_pair, w_down, core, reps
    )
    h2s.append(h2_last)
    acts, boths = (acts, acts1), (boths, boths1)
    second0, second1 = rep_scatter(second0), rep_scatter(second1)
    down_grad = grad((after(acts[0], mixed1), acts[1]), ups)
    down_sends = sends(down_grad[:units].reshape(grps, piece, width))
    pair_grad = grad([after(h2s[0], second0, *down_sends)] + h2s[1:], boths)
    mixed0, mixed1 = rep_scatter(mixed0), rep_scatter(mixed1)
    pair_sends = sends(pair_grad.reshape(grps, own, 2 * lanes))
    if fast:
        down_turns = turned(down_sends)
        down_turns[1] = after(down_turns[1], *pair_sends)
        down_own = total(down_turns).astype(BF16)
        second1 = after(second1, down_own)
    else:
        down_own = total(turned(down_sends)).astype(BF16)
        pair_own = total(turned(pair_sends)).astype(BF16)

    block = 4 * width // reps
    split = width // block
    if fast:
        d_resid, d_branch, d_c, d_conv, local_mid = mid_backward(
            second0, second1, cotangent, normed_two, scale_two, gain_two[None], right, conv, c_part
        )
        local_mid = local_mid[0]
        later = from_behind(d_conv[: taps - 1], "grp", -1)
        near = [turn(after(pair_sends[k], later), k) for k in (1, 3)]
        d_all, local_taps = taps_backward(
            d_conv, later, taps_f, b_part, x_part, gated, earlier, d_c, d_branch, block
        )
        local_taps = list(local_taps)
    else:
        d_second = jnp.concatenate([second0, second1], axis=0).astype(F32)
        local_mid = jnp.sum(d_second * normed_two, axis=0)
        d_normed_two = d_second * gain_two
        d_resid = cotangent.astype(F32) + scale_two * (
            d_normed_two - normed_two * jnp.mean(d_normed_two * normed_two, axis=-1, keepdims=True)
        )
        d_branch = d_resid.astype(BF16)
        d_z = right_transposed(d_branch, w_out)
        d_c = d_z * conv
        d_conv = d_z * c_part
        later = from_behind(d_conv[: taps - 1], "grp", -1)
        padded_back = jnp.concatenate([d_conv, later], axis=0)
        d_gated = taps_f[0] * padded_back[taps - 1 : taps - 1 + rows]
        for tap in range(1, taps):
            ahead = taps - 1 - tap
            d_gated = d_gated + taps_f[tap] * padded_back[ahead : ahead + rows]
        padded = jnp.concatenate([earlier, gated], axis=0)
        local_taps = [jnp.sum(d_conv * padded[tap : tap + rows], axis=0) for tap in range(taps)]
        d_all = jnp.concatenate([d_gated * x_part, d_c, d_gated * b_part], axis=1).astype(BF16)
        d_all = jnp.concatenate([d_all, d_branch], axis=1)
        d_all = d_all.reshape(rows, reps, block).swapaxes(0, 1)

    lefts = jnp.stack([h_low, z_low])
    if fast:
        places = lambda *ms: jnp.stack([rep ^ m for m in ms])
        grads_one = block_grads(places(7, 3), lefts, d_all)
        flips_one = [flip(value, 1) for value in grads_one]
        grads_two = block_grads(places(5, 1), lefts, after(d_all, *grads_one))
        flips_two = [flip(value, 1) for value in grads_two]
        d_all = after(d_all, *grads_two)
        up6, low6, up2, low2 = block_grads(
            places(6, 2), lefts, d_all, flips_one, (BF16, BF16, BF16, F32)
        )
        one6, two6, one2 = flip(up6, 2), flip(low6, 4), flip(up2, 2)
        d_all = after(d_all, up6)
        up4, low4, up0, low0 = block_grads(
            places(4, 0), lefts, d_all, flips_two, (F32, BF16, F32, F32)
        )
        two4 = flip(low4, 4)
        d_all = after(d_all, up4, down_own)
    else:
        summed = jnp.concatenate(
            [
                left_product(h_low if j < 3 * split else z_low, d_all[j]).astype(BF16)
                for j in range(reps)
            ]
        )
        summed = lax.psum_scatter(summed, "rep", scatter_dimension=0, tiled=True)

    d_left = jnp.concatenate([d_all[j] for j in range(2 * split)], axis=1)
    d_right = jnp.concatenate([d_all[2 * split + j] for j in range(split)], axis=1)
    d_hidden = right_transposed(d_left, left) + right_transposed(d_right, w_x)
    normed = tokens.astype(F32) * scale_one
    local_in = jnp.sum(d_hidden * normed, axis=0)
    d_normed = d_hidden * gain_one
    input_grad = d_resid + scale_one * (
        d_normed - normed * jnp.mean(d_normed * normed, axis=-1, keepdims=True)
    )
    sums = jnp.stack([local_in, local_mid] + local_taps)
    if fast:
        one6, two6 = after(one6, input_grad, *near), after(two6, input_grad, *near)
        one4_send = (up4 + one6.astype(F32)).astype(BF16)
        two2_send = (low2 + two6.astype(F32)).astype(BF16)
        one4, two2 = flip(one4_send, 4), flip(two2_send, 2)
        far = turn(after(pair_sends[2], one4_send, two2_send), 2)
        one0 = up0 + one2.astype(F32) + one4.astype(F32)
        two0 = low0 + two4.astype(F32) + two2.astype(F32)
        summed = jnp.concatenate([one0, two0], axis=0).astype(BF16)
        conv_sends = sends(summed.reshape(grps, own, block))
        conv_near = [turn(conv_sends[k], k) for k in (1, 3)]
        pair_own = total([after(pair_sends[0], *conv_sends), near[0], far, near[1]]).astype(BF16)
        sums = after(sums, *conv_sends)
        for bit in (1, 2, 4):
            sums = sums + flip(sums, bit)
        conv_far = turn(after(conv_sends[2], *conv_near), 2)
        sums = after(sums, *conv_near)
        owned = total(turned(sends(sums.reshape(2 + taps, grps, own).swapaxes(0, 1))))
        conv_turns = [conv_sends[0], conv_near[0], conv_far, conv_near[1]]
    else:
        sums = lax.psum(sums, "rep").reshape(2 + taps, grps, own).swapaxes(0, 1)
        owned = total(turned(sends(sums)))
        conv_turns = turned(sends(summed.reshape(grps, own, block)))
    down_full = rep_gather(down_own).reshape(-1, width).astype(F32)
    pair_full = rep_gather(pair_own)
    mixed = jnp.concatenate([mixed0, mixed1], axis=0).astype(F32)
    if fast:
        mixed = after(mixed, *conv_sends)
    mixed = (resid + mixed).astype(BF16)
    if fast:
        conv_turns[1] = after(conv_turns[1], mixed, down_full, owned)
        parts = first(total(conv_turns).astype(BF16))
        came = swap(parts, (2, 4))
        parts = second(parts, came)
        came = swap(parts, (4, 2))
        gate_full, up_full = spread(pair_full, grps, piece)
        conv_same = third(parts, [after(value, gate_full, up_full) for value in came])
    else:
        conv_same = chips_gather(total(conv_turns).astype(BF16))
        gate_full, up_full = spread(pair_full, grps, piece)
    conv_other = flip(conv_same, 1)
    in_full, out_full = unblock((rep & 1).reshape(1), conv_same, conv_other, width)
    return (
        mixed,
        input_grad,
        owned[0],
        in_full,
        owned[2:].T,
        out_full,
        owned[1],
        gate_full,
        up_full,
        down_full,
    )


def solution(mesh):
    placed = (
        P(("rep", "grp"), None),
        P("grp"),
        P("grp", None),
        P("grp", None),
        P("grp", None),
        P("grp"),
        P("grp", None),
        P("grp", None),
        P("grp", None),
        P(("rep", "grp"), None),
    )
    return jax.shard_map(
        shards,
        mesh=mesh,
        in_specs=placed,
        out_specs=(
            P(("rep", "grp"), None),
            P(("rep", "grp"), None),
            P("grp"),
            P("grp", None),
            P("grp", None),
            P("grp", None),
            P("grp"),
            P("grp", None),
            P("grp", None),
            P("grp", None),
        ),
        check_vma=False,
    )
```

```python
import functools

import jax
import jax.numpy as jnp
from jax import lax
from jax.experimental import pallas as pl
from jax.experimental.pallas import tpu as pltpu
from jax.sharding import PartitionSpec as P

EPS = 1e-05
F32, BF16 = jnp.float32, jnp.bfloat16
LIGHT = pl.CostEstimate(flops=1, bytes_accessed=1, transcendentals=0)


def after(value, *others):
    return lax.optimization_barrier((value,) + others)[0]


def from_behind(value, axis, steps):
    count = lax.axis_size(axis)
    first, last = (max(0, -steps), min(count, count - steps))
    return lax.ppermute(value, axis, [(source, source + steps) for source in range(first, last)])


def product(left, right):
    return jnp.dot(left, right, preferred_element_type=F32)


def left_product(left, right):
    return lax.dot_general(left, right, (((0,), (0,)), ((), ())), preferred_element_type=F32)


def right_transposed(left, right):
    return lax.dot_general(left, right, (((1,), (1,)), ((), ())), preferred_element_type=F32)


def turn(value, places):
    count = lax.axis_size("grp")
    return lax.ppermute(value, "grp", [(i, (i + places) % count) for i in range(count)])


def behind(places):
    count = lax.axis_size("grp")
    return lax.rem(lax.axis_index("grp") - places + count, count)


def placed(values):
    out = jnp.zeros((len(values),) + values[0].shape, values[0].dtype)
    for places, value in enumerate(values):
        out = lax.dynamic_update_index_in_dim(out, value, behind(places), 0)
    return out


def sends(parts):
    return [
        lax.dynamic_index_in_dim(parts, behind(-places), 0, keepdims=False)
        for places in range(lax.axis_size("grp"))
    ]


def turned(parts):
    return parts[:1] + [turn(part, places + 1) for places, part in enumerate(parts[1:])]


def total(parts):
    return sum(part.astype(F32) for part in parts)


def flip(value, bit):
    return lax.ppermute(value, "rep", [(i, i ^ bit) for i in range(lax.axis_size("rep"))])


def pair(mine, other, bit, axis):
    low = (lax.axis_index("rep") & bit) == 0
    return jnp.stack([jnp.where(low, mine, other), jnp.where(low, other, mine)], axis)


def same_core():
    chips = lax.axis_size("rep") // 2
    return [[2 * chip + core for chip in range(chips)] for core in range(2)]


def chips_gather(value):
    return lax.all_gather(value, "rep", axis=0, axis_index_groups=same_core())


def chips_gather_two(one, two):
    if lax.axis_size("rep") != 8:
        return chips_gather(one), chips_gather(two)
    one_x, two_y = flip(one, 2), flip(two, 4)
    one, two = pair(one, one_x, 2, 0), pair(two, two_y, 4, 0)
    one_y, two_x = flip(one, 4), flip(two, 2)
    one, two = pair(one, one_y, 4, 0), pair(two, two_x, 2, 1)
    return one.reshape((4,) + one.shape[2:]), two.reshape((4,) + two.shape[2:])


def chips_gather_steps(value):
    half = value.shape[-1] // 2
    return jnp.concatenate(chips_gather_two(value[..., :half], value[..., half:]), axis=-1)


def chips_scatter(value):
    return lax.psum_scatter(
        value, "rep", scatter_dimension=0, tiled=True, axis_index_groups=same_core()
    )


def chips_scatter_steps(value):
    if lax.axis_size("rep") != 8:
        return chips_scatter(value).astype(F32)
    rep = lax.axis_index("rep")
    rows, half = value.shape[0] // 4, value.shape[1] // 2

    def split(part, bit, axis):
        mine = jnp.where((rep & bit) == 0, 0, 1)
        pick = lambda i: lax.dynamic_index_in_dim(part, i, axis, keepdims=False)
        return pick(mine).astype(F32), pick(1 - mine).astype(BF16)

    value = value.reshape(2, 2, rows, 2 * half)
    one, send_one = split(value[..., :half], 2, 1)
    two, send_two = split(value[..., half:], 4, 0)
    one, two = one + flip(send_one, 2).astype(F32), two + flip(send_two, 4).astype(F32)
    one, send_one = split(one, 4, 0)
    two, send_two = split(two, 2, 0)
    one, two = one + flip(send_one, 4).astype(F32), two + flip(send_two, 2).astype(F32)
    return jnp.concatenate([one, two], axis=-1)


def rep_scatter(value):
    return lax.psum_scatter(value, "rep", scatter_dimension=0, tiled=True)


def rep_gather(value):
    return lax.all_gather(value, "rep", axis=0)


def spread_kernel(piece, padded, groups, pair_ref, gate_ref, up_ref):
    reps, _, lanes = pair_ref.shape
    for start, out_ref in ((0, gate_ref), (lanes // 2, up_ref)):
        for j in range(groups):
            for rep in range(reps):
                place, source = (j * reps + rep) * piece, start + j * padded
                out_ref[:, place : place + piece] = pair_ref[
                    rep, :, source : source + piece
                ].astype(F32)


def spread(part, groups, piece, padded):
    reps, rows, lanes = part.shape
    hidden = reps * groups * piece
    tile = 64
    return pl.pallas_call(
        functools.partial(spread_kernel, piece, padded, groups),
        grid=(rows // tile,),
        in_specs=[pl.BlockSpec((reps, tile, lanes), lambda i: (0, i, 0))],
        out_specs=[pl.BlockSpec((tile, hidden), lambda i: (i, 0))] * 2,
        out_shape=[jax.ShapeDtypeStruct((rows, hidden), F32)] * 2,
        compiler_params=pltpu.CompilerParams(vmem_limit_bytes=60 * 2**20),
        cost_estimate=pl.CostEstimate(flops=0, bytes_accessed=rows * hidden * 12, transcendentals=0),
    )(part)


def place_kernel(count, steps, table_ref, *refs):
    del table_ref
    step = pl.program_id(0)
    left_ref, right_ref = refs[-2:]
    for k in range(count):

        @pl.when((step >= k * steps) & (step < (k + 1) * steps))
        def _(k=k):
            left_ref[...] = refs[2 * k][0, 0]
            right_ref[...] = refs[2 * k + 1][0, 0]


def place_weights(left, right, pieces, cores, near, rep, grp):
    _, turns, cut, cols = pieces[0].shape
    own = left.shape[0] // (turns + 1)
    x, y = (rep >> 1) & 1, rep >> 2
    if not near:
        x, y = 1 - x, 1 - y
    rows = lambda places, chip, core: behind(places) * (own // cut) + 2 * chip + core
    table = jnp.stack(
        [
            rows(places, chip, core)
            for which in range(2)
            for core in cores
            for line in range(2)
            for places in range(1, turns + 1)
            for chip in ((2 * y + line, 2 * line + x)[which],)
        ]
    )
    count, steps = len(cores), 2 * turns

    def came(k):
        def index(i, table):
            step = jnp.clip(i - k * steps, 0, steps - 1)
            return (step // turns, step % turns, 0, 0)

        return pl.BlockSpec((1, 1, cut, cols), index)

    anywhere = pl.BlockSpec(memory_space=pl.ANY)
    total_steps = count * steps
    return pl.pallas_call(
        lambda table_ref, *refs: place_kernel(count, steps, table_ref, *refs[2:]),
        grid_spec=pltpu.PrefetchScalarGridSpec(
            num_scalar_prefetch=1,
            grid=(total_steps,),
            in_specs=[anywhere] * 2 + [came(k // 2) for k in range(2 * count)],
            out_specs=[
                pl.BlockSpec((cut, cols), lambda i, table: (table[i], 0)),
                pl.BlockSpec((cut, cols), lambda i, table: (table[total_steps + i], 0)),
            ],
        ),
        out_shape=[jax.ShapeDtypeStruct(left.shape, BF16)] * 2,
        input_output_aliases={1: 0, 2: 1},
        compiler_params=pltpu.CompilerParams(vmem_limit_bytes=60 * 2**20),
        cost_estimate=LIGHT,
    )(table, left, right, *pieces)


def in_kernel(tokens_ref, gain_ref, b_ref, c_ref, x_ref, h_ref, scale_ref, b_out, c_out, x_out, edge_ref):
    @pl.when(pl.program_id(0) == 0)
    def _():
        inputs = tokens_ref[...].astype(F32)
        scale = lax.rsqrt(jnp.mean(inputs * inputs, axis=-1, keepdims=True) + EPS)
        scale_ref[...] = scale
        h_ref[...] = (inputs * scale * gain_ref[...]).astype(BF16)

    h_low = h_ref[...]
    b_part = product(h_low, b_ref[...])
    x_part = product(h_low, x_ref[...])
    b_out[...] = b_part
    x_out[...] = x_part
    c_out[...] = product(h_low, c_ref[...])
    edge_ref[...] = (b_part * x_part)[-edge_ref.shape[0] :]


def in_forward(tokens, gain, left, right):
    rows, width = tokens.shape
    cols = 256
    count = width // cols
    whole = pl.BlockSpec((rows, width), lambda i: (0, 0))
    column = pl.BlockSpec((rows, cols), lambda i: (0, i))
    weight = lambda start: pl.BlockSpec((width, cols), lambda i: (0, start + i))
    part = jax.ShapeDtypeStruct((rows, width), F32)
    return pl.pallas_call(
        in_kernel,
        grid=(count,),
        in_specs=[
            whole,
            pl.BlockSpec((1, width), lambda i: (0, 0)),
            weight(0),
            weight(count),
            weight(0),
        ],
        out_specs=[
            whole,
            pl.BlockSpec((rows, 1), lambda i: (0, 0)),
            column,
            column,
            column,
            pl.BlockSpec((8, cols), lambda i: (0, i)),
        ],
        out_shape=[
            jax.ShapeDtypeStruct((rows, width), BF16),
            jax.ShapeDtypeStruct((rows, 1), F32),
            part,
            part,
            part,
            jax.ShapeDtypeStruct((8, width), F32),
        ],
        compiler_params=pltpu.CompilerParams(vmem_limit_bytes=60 * 2**20),
        cost_estimate=LIGHT,
    )(tokens, gain, left, left, right)


def out_kernel(
    tokens_ref, gain_ref, taps_ref, earlier_ref, b_ref, c_ref, x_ref, w_ref,
    gated_ref, conv_ref, z_ref, resid_ref, normed_ref, scale_ref, h2_ref, sum_ref,
):
    step = pl.program_id(0)
    rows = b_ref.shape[0]
    gated = b_ref[...] * x_ref[...]
    gated_ref[...] = gated
    padded = jnp.concatenate([earlier_ref[...], gated], axis=0)
    conv = taps_ref[0:1] * padded[0:rows]
    for tap in range(1, taps_ref.shape[0]):
        conv = conv + taps_ref[tap : tap + 1] * padded[tap : tap + rows]
    conv_ref[...] = conv
    z_low = (c_ref[...] * conv).astype(BF16)
    z_ref[...] = z_low

    @pl.when(step == 0)
    def _():
        sum_ref[...] = tokens_ref[...].astype(F32)

    sum_ref[...] += product(z_low, w_ref[...])

    @pl.when(step == pl.num_programs(0) - 1)
    def _():
        resid = sum_ref[...]
        resid_ref[...] = resid
        scale = lax.rsqrt(jnp.mean(resid * resid, axis=-1, keepdims=True) + EPS)
        scale_ref[...] = scale
        normed = resid * scale
        normed_ref[...] = normed
        h2_ref[...] = (normed * gain_ref[...]).astype(BF16)


def out_forward(tokens, gain, taps_f, earlier, b_part, c_part, x_part, right):
    rows, width = tokens.shape
    cols = 256
    whole = pl.BlockSpec((rows, width), lambda i: (0, 0))
    column = lambda n: pl.BlockSpec((n, cols), lambda i: (0, i))
    full = lambda kind: jax.ShapeDtypeStruct((rows, width), kind)
    return pl.pallas_call(
        out_kernel,
        grid=(width // cols,),
        in_specs=[
            whole,
            pl.BlockSpec((1, width), lambda i: (0, 0)),
            column(taps_f.shape[0]),
            column(earlier.shape[0]),
            column(rows),
            column(rows),
            column(rows),
            pl.BlockSpec((cols, width), lambda i: (i, 1)),
        ],
        out_specs=[
            column(rows),
            column(rows),
            column(rows),
            whole,
            whole,
            pl.BlockSpec((rows, 1), lambda i: (0, 0)),
            whole,
        ],
        out_shape=[
            full(F32),
            full(F32),
            full(BF16),
            full(F32),
            full(F32),
            jax.ShapeDtypeStruct((rows, 1), F32),
            full(BF16),
        ],
        scratch_shapes=[pltpu.VMEM((rows, width), F32)],
        compiler_params=pltpu.CompilerParams(vmem_limit_bytes=60 * 2**20),
        cost_estimate=LIGHT,
    )(tokens, gain, taps_f, earlier, b_part, c_part, x_part, right)


def mid_kernel(
    second0_ref, second1_ref, up_ref, normed_ref, scale_ref, gain_ref, w_ref, conv_ref, c_ref,
    resid_ref, branch_ref, d_c_ref, d_conv_ref, sum_ref,
):
    step, half_steps = pl.program_id(0), pl.num_programs(0) // 2

    @pl.when(step == 0)
    def _():
        sum_ref[...] = jnp.zeros_like(sum_ref)

    d_second = jnp.where(step < half_steps, second0_ref[...], second1_ref[...]).astype(F32)
    normed = normed_ref[...]
    both = d_second * normed
    sum_ref[...] += jnp.sum(both, axis=0, keepdims=True)
    d_normed = d_second * gain_ref[...]
    mean = jnp.mean(d_normed * normed, axis=-1, keepdims=True)
    d_resid = up_ref[...].astype(F32) + scale_ref[...] * (d_normed - normed * mean)
    resid_ref[...] = d_resid
    branch = d_resid.astype(BF16)
    branch_ref[...] = branch
    d_z = right_transposed(branch, w_ref[...])
    d_c_ref[...] = (d_z * conv_ref[...]).astype(BF16)
    d_conv_ref[...] = d_z * c_ref[...]


def mid_backward(second0, second1, upstream, normed, scale, gain, right, conv, c_part):
    rows, width = normed.shape
    tile = rows // 2
    steps = 2
    row = pl.BlockSpec((tile, width), lambda i: (i, 0))
    first = pl.BlockSpec((tile, width), lambda i: (jnp.minimum(i, steps // 2 - 1), 0))
    last = pl.BlockSpec((tile, width), lambda i: (jnp.maximum(i - steps // 2, 0), 0))
    line = pl.BlockSpec((1, width), lambda i: (0, 0))
    return pl.pallas_call(
        mid_kernel,
        grid=(steps,),
        in_specs=[
            first,
            last,
            row,
            row,
            pl.BlockSpec((tile, 1), lambda i: (i, 0)),
            line,
            pl.BlockSpec((width, width), lambda i: (0, 1)),
            row,
            row,
        ],
        out_specs=[row, row, row, row, line],
        out_shape=[
            jax.ShapeDtypeStruct((rows, width), F32),
            jax.ShapeDtypeStruct((rows, width), BF16),
            jax.ShapeDtypeStruct((rows, width), BF16),
            jax.ShapeDtypeStruct((rows, width), F32),
            jax.ShapeDtypeStruct((1, width), F32),
        ],
        compiler_params=pltpu.CompilerParams(vmem_limit_bytes=60 * 2**20),
        cost_estimate=LIGHT,
    )(second0, second1, upstream, normed, scale, gain, right, conv, c_part)


def taps_kernel(d_conv_ref, later_ref, taps_ref, b_ref, x_ref, u_ref, earlier_ref, d_c_ref, branch_ref, all_ref, sum_ref):
    rows = d_conv_ref.shape[0]
    taps = taps_ref.shape[0]
    d_conv = d_conv_ref[...]
    after_it = jnp.concatenate([d_conv, later_ref[...]], axis=0)
    before_it = jnp.concatenate([earlier_ref[...], u_ref[...]], axis=0)
    d_gated = jnp.zeros_like(d_conv)
    for tap in range(taps):
        ahead = taps - 1 - tap
        d_gated = d_gated + taps_ref[tap : tap + 1] * after_it[ahead : ahead + rows]
        sum_ref[tap : tap + 1] = jnp.sum(d_conv * before_it[tap : tap + rows], axis=0, keepdims=True)
    all_ref[0, 0] = (d_gated * x_ref[...]).astype(BF16)
    all_ref[1, 0] = d_c_ref[...]
    all_ref[2, 0] = (d_gated * b_ref[...]).astype(BF16)
    all_ref[3, 0] = branch_ref[...]


def taps_backward(d_conv, later, taps_f, b_part, x_part, gated, earlier, d_c, branch, block):
    rows, width = d_conv.shape
    taps = taps_f.shape[0]
    cols = 256
    per = block // cols
    column = lambda n: pl.BlockSpec((n, cols), lambda i: (0, i))
    d_all, sums = pl.pallas_call(
        taps_kernel,
        grid=(width // cols,),
        in_specs=[
            column(rows),
            column(taps - 1),
            column(taps),
            column(rows),
            column(rows),
            column(rows),
            column(taps - 1),
            column(rows),
            column(rows),
        ],
        out_specs=[
            pl.BlockSpec((4, 1, rows, cols), lambda i: (0, i // per, 0, i % per)),
            column(taps),
        ],
        out_shape=[
            jax.ShapeDtypeStruct((4, width // block, rows, block), BF16),
            jax.ShapeDtypeStruct((taps, width), F32),
        ],
        compiler_params=pltpu.CompilerParams(vmem_limit_bytes=60 * 2**20),
        cost_estimate=LIGHT,
    )(d_conv, later, taps_f, b_part, x_part, gated, earlier, d_c, branch)
    return d_all.reshape(-1, rows, block), sums


def ffn_kernel(core_ref, same_ref, other_ref, up_same_ref, up_other_ref, pair_ref, down_ref, *refs):
    del core_ref
    act_ref, both_ref, second_ref, mixed_ref = refs[-4:]
    lanes, width = down_ref.shape
    first_half = pl.program_id(0) < pl.num_programs(0) // 2
    rows = lambda ref: ref[...].reshape(-1, width)
    h2 = jnp.where(first_half, rows(same_ref), rows(other_ref))
    up_g = jnp.where(first_half, rows(up_same_ref), rows(up_other_ref))
    both = product(h2, pair_ref[...])
    gate, upper = both[:, :lanes], both[:, lanes:]
    sigma = jax.nn.sigmoid(gate)
    swish = gate * sigma
    act = (swish * upper).astype(BF16)
    act_ref[...] = act
    d_act = right_transposed(up_g, down_ref[...])
    d_gate = (d_act * upper * sigma * (1.0 + gate * (1.0 - sigma))).astype(BF16)
    d_upper = (d_act * swish).astype(BF16)
    both_ref[...] = jnp.concatenate([d_gate, d_upper], axis=1).reshape(both_ref.shape)
    second = right_transposed(both_ref[...].reshape(-1, 2 * lanes), pair_ref[...]).astype(BF16)
    second_ref[...] = second.reshape(second_ref.shape)
    mixed_ref[...] = product(act, down_ref[...]).astype(BF16).reshape(mixed_ref.shape)


def ffn(h2s, ups, w_pair, w_down, core, which, filled=()):
    chips, tile, width = ups[0].shape
    tile //= 2
    lanes = w_down.shape[0]
    natural = len(h2s) == 1
    per = 2
    steps = chips // per
    turns = [lambda i: jnp.minimum(i, steps - 1), lambda i: jnp.maximum(i - steps, 0)]
    side = lambda i, core: jnp.where(i < steps, core[0], 1 - core[0])
    plain = lambda n: pl.BlockSpec((per * tile, n), lambda i, core: (i, 0))
    ordered = lambda n: pl.BlockSpec(
        (per, 1, tile, n), lambda i, core: (i % steps, side(i, core), 0, 0)
    )
    full = lambda w: pl.BlockSpec(w.shape, lambda i, core: (0, 0), pipeline_mode=pl.Buffered(1))
    if natural:
        h2s = [h2s[0].reshape(chips, 2, tile, width)] * 2
        h2_specs = [
            pl.BlockSpec((per, 1, tile, width), lambda i, core, k=k: (turns[k](i), core[0] ^ k, 0, 0))
            for k in range(2)
        ]
    else:
        h2s = [value.reshape(chips, tile, width) for value in h2s]
        h2_specs = [
            pl.BlockSpec((per, tile, width), lambda i, core, k=k: (turns[k](i), 0, 0))
            for k in range(2)
        ]
    tokens = 2 * chips * tile
    placed_ = lambda n: jax.ShapeDtypeStruct((chips, 2, tile, n), BF16)
    acts, boths, second, mixed = pl.pallas_call(
        ffn_kernel,
        grid_spec=pltpu.PrefetchScalarGridSpec(
            num_scalar_prefetch=1,
            grid=(2 * steps,),
            in_specs=h2_specs
            + [
                pl.BlockSpec((per, tile, width), lambda i, core, at=at: (at(i), which, 0))
                for at in turns
            ]
            + [full(w_pair), full(w_down)]
            + [pl.BlockSpec(memory_space=pl.ANY) for _ in filled],
            out_specs=[
                plain(lanes),
                ordered(2 * lanes) if natural else plain(2 * lanes),
                ordered(width),
                pl.BlockSpec(
                    (per, 1, 1, tile, width),
                    lambda i, core: (i % steps, side(i, core), which, 0, 0),
                ),
            ],
        ),
        out_shape=[
            jax.ShapeDtypeStruct((tokens, lanes), BF16),
            placed_(2 * lanes) if natural else jax.ShapeDtypeStruct((tokens, 2 * lanes), BF16),
            placed_(width),
            jax.ShapeDtypeStruct((chips, 2, 2, tile, width), BF16),
        ],
        input_output_aliases={7: 3} if filled else {},
        compiler_params=pltpu.CompilerParams(vmem_limit_bytes=60 * 2**20),
        cost_estimate=pl.CostEstimate(
            flops=17 * tokens * width * lanes, bytes_accessed=0, transcendentals=0
        ),
    )(core, *h2s, *ups, w_pair, w_down, *filled)
    return acts, boths.reshape(tokens, -1), second.reshape(tokens, width), mixed


def grad_kernel(parts, lefts_count, *refs):
    lefts, rights, out_ref, total_ref = (
        refs[:lefts_count],
        refs[lefts_count:-2],
        refs[-2],
        refs[-1],
    )
    step = pl.program_id(0)

    @pl.when(step == 0)
    def _():
        total_ref[...] = jnp.zeros_like(total_ref)

    for start, stop, left, right in parts:

        @pl.when((step >= start) & (step < stop))
        def _(left=left, right=right):
            value = rights[right][...]
            value = value.reshape(-1, value.shape[-1])
            total_ref[...] += left_product(lefts[left][...], value)

    @pl.when(step == pl.num_programs(0) - 1)
    def _():
        out_ref[...] = total_ref[...].astype(BF16)


def grad(lefts, rights, halves=None):
    tile = 480
    n, m = lefts[0].shape[1], rights[0].shape[-1]

    def cuts(arrays):
        out = [0]
        for array in arrays:
            out.append(out[-1] + array.size // array.shape[-1] // tile // (array.ndim - 1))
        return out

    left_cuts, right_cuts = cuts(lefts), cuts(rights)
    edges = sorted(set(left_cuts + right_cuts))
    find = lambda which, step: max(k for k in range(len(which) - 1) if which[k] <= step)
    parts = [
        (start, stop, find(left_cuts, start), find(right_cuts, start))
        for start, stop in zip(edges, edges[1:])
    ]

    def spec(which, k, array):
        at = lambda i: jnp.clip(i, which[k], which[k + 1] - 1) - which[k]
        if array.ndim == 2:
            return pl.BlockSpec((tile, array.shape[1]), lambda i: (at(i), 0))
        half = array.shape[1] // 2
        return pl.BlockSpec((tile // half, half, array.shape[2]), lambda i: (at(i), halves[k], 0))

    return pl.pallas_call(
        functools.partial(grad_kernel, parts, len(lefts)),
        grid=(edges[-1],),
        in_specs=[spec(left_cuts, k, array) for k, array in enumerate(lefts)]
        + [spec(right_cuts, k, array) for k, array in enumerate(rights)],
        out_specs=pl.BlockSpec((n, m), lambda i: (0, 0)),
        out_shape=jax.ShapeDtypeStruct((n, m), BF16),
        scratch_shapes=[pltpu.VMEM((n, m), F32)],
        compiler_params=pltpu.CompilerParams(vmem_limit_bytes=60 * 2**20),
        cost_estimate=pl.CostEstimate(flops=3 * tile * edges[-1] * n * m, bytes_accessed=0, transcendentals=0),
    )(*lefts, *rights)


def block_kernel(count, kept, places_ref, *refs):
    del places_ref
    lefts, rights, refs = refs[:count], refs[count : 2 * count], refs[2 * count :]
    for k in range(count):
        total_ = left_product(lefts[k][0], rights[k][0])
        if not kept:
            refs[k][...] = total_.astype(BF16)
            continue
        total_ = total_ + refs[k][...].astype(F32)
        for which in range(2):

            @pl.when(pl.program_id(0) == which)
            def _(k=k, which=which, total_=total_):
                ref = refs[count + 2 * k + which]
                ref[...] = total_.astype(ref.dtype)


def block_grads(places, lefts, rights, came=(), kept=()):
    count = places.shape[0]
    rows, width = lefts.shape[1:]
    blocks, _, block = rights.shape
    branch = blocks - blocks // 4
    left = lambda k: pl.BlockSpec(
        (1, rows, width // 2), lambda i, places: ((places[k] >= branch).astype(jnp.int32), 0, i)
    )
    right = lambda k: pl.BlockSpec((1, rows, block), lambda i, places: (places[k], 0, 0))
    moving = pl.BlockSpec((width // 2, block), lambda i, places: (i, 0))
    fixed = pl.BlockSpec((width // 2, block), lambda i, places: (0, 0))
    if kept:
        outs = [jax.ShapeDtypeStruct((width // 2, block), kind) for kind in kept]
    else:
        outs = [jax.ShapeDtypeStruct((width, block), BF16)] * count
    return pl.pallas_call(
        functools.partial(block_kernel, count, bool(kept)),
        grid_spec=pltpu.PrefetchScalarGridSpec(
            num_scalar_prefetch=1,
            grid=(2,),
            in_specs=[left(k) for k in range(count)]
            + [right(k) for k in range(count)]
            + [moving for _ in came],
            out_specs=[fixed if kept else moving for _ in outs],
        ),
        out_shape=outs,
        compiler_params=pltpu.CompilerParams(vmem_limit_bytes=40 * 2**20),
        cost_estimate=LIGHT,
    )(places, *([lefts] * count), *([rights] * count), *came)


def unblock_kernel(core_ref, same_ref, other_ref, in_ref, out_ref):
    chips, _, block = same_ref.shape
    first = core_ref[0] == 0
    for chip in range(chips):
        same, other = same_ref[chip].astype(F32), other_ref[chip].astype(F32)
        for core, value in enumerate((jnp.where(first, same, other), jnp.where(first, other, same))):
            place = (2 * chip + core) * block
            if place < in_ref.shape[1]:
                in_ref[:, place : place + block] = value
            else:
                place -= in_ref.shape[1]
                out_ref[:, place : place + block] = value


def unblock(core, same, other, width):
    chips, rows, block = same.shape
    tile = 96
    spec = pl.BlockSpec((chips, tile, block), lambda i, core: (0, i, 0))
    return pl.pallas_call(
        unblock_kernel,
        grid_spec=pltpu.PrefetchScalarGridSpec(
            num_scalar_prefetch=1,
            grid=(rows // tile,),
            in_specs=[spec, spec],
            out_specs=[pl.BlockSpec((tile, n), lambda i, core: (i, 0)) for n in (3 * width, width)],
        ),
        out_shape=[jax.ShapeDtypeStruct((rows, n), F32) for n in (3 * width, width)],
        compiler_params=pltpu.CompilerParams(vmem_limit_bytes=60 * 2**20),
        cost_estimate=pl.CostEstimate(flops=0, bytes_accessed=24 * rows * width, transcendentals=0),
    )(core, same, other)


def shards(
    tokens,
    norm_in,
    in_weight,
    conv_weight,
    out_weight,
    norm_mid,
    gate_weight,
    up_weight,
    down_weight,
    cotangent,
):
    reps, grps = lax.axis_size("rep"), lax.axis_size("grp")
    rep, grp = lax.axis_index("rep"), lax.axis_index("grp")
    chips = reps // 2
    low_core = (rep & 1) == 0
    rows, width = tokens.shape
    taps = conv_weight.shape[1]
    own = in_weight.shape[0]
    hidden = gate_weight.shape[1]
    piece = hidden // (reps * grps)
    padded = -(-piece // 16) * 16
    units = padded * grps
    lanes = -(-units // 128) * 128
    half = rows // 2

    def columns(weight):
        gap, parts = jnp.zeros((own, padded - piece), BF16), []
        for j in range(grps):
            place = j * (hidden // grps) + rep * piece
            parts += [lax.dynamic_slice(weight, (0, place), (own, piece)), gap]
        return jnp.concatenate(parts + [jnp.zeros((own, lanes - units), BF16)], axis=1)

    pair_piece = jnp.concatenate([columns(gate_weight), columns(up_weight)], axis=1)
    down_piece = lax.dynamic_slice_in_dim(down_weight, rep * piece, piece, 0)
    down_piece = jnp.pad(down_piece, ((0, padded - piece), (0, 0)))
    cut = own // reps
    gains = jnp.concatenate([norm_in[None], norm_mid[None], conv_weight.T], axis=0)
    sent = jnp.concatenate(
        [
            lax.dynamic_slice_in_dim(in_weight, rep * cut, cut, 0),
            lax.dynamic_slice_in_dim(out_weight, rep * cut, cut, 0),
        ],
        axis=1,
    )
    fast = reps == 8 and grps == 4
    if fast:
        def first(value):
            half_cols = value.shape[-1] // 2
            return [value[..., :half_cols], value[..., half_cols:]]

        def swap(values, bits):
            return [flip(value, bit) for value, bit in zip(values, bits)]

        def second(values, came):
            return [pair(values[0], came[0], 2, 0), pair(values[1], came[1], 4, 0)]

        def third(values, came):
            both = [pair(values[0], came[0], 4, 0), pair(values[1], came[1], 2, 1)]
            return jnp.concatenate([value.reshape((4,) + value.shape[2:]) for value in both], axis=-1)

        side = -(-gains.size // (cut * 128)) * 128
        gains = jnp.pad(gains.reshape(-1), (0, cut * side - gains.size)).reshape(cut, side)
        sent = jnp.concatenate([sent, gains], axis=1)
        near = [turn(sent, 1), turn(sent, 3)]
        ups = first(cotangent)
        left = jnp.zeros((width, 2 * width), BF16)
        left = lax.dynamic_update_slice(left, in_weight[:, : 2 * width], (grp * own, 0))
        right = jnp.zeros((width, 2 * width), BF16)
        right = lax.dynamic_update_slice(right, in_weight[:, 2 * width :], (grp * own, 0))
        right = lax.dynamic_update_slice(right, out_weight, (grp * own, width))
        came = [after(value, pair_piece, left, right, *near) for value in swap(ups, (2, 4))]
        ups = second(ups, came)
        far = turn(after(sent, *near), 2)
        w_pair = lax.all_gather(after(pair_piece, far), "grp", axis=0, tiled=True)
        hops = [after(near[0], *ups), far, near[1]]
        small = placed([gains] + [value[:, 4 * width :] for value in hops])
        small = small.reshape(grps, -1)[:, : (2 + taps) * own].reshape(grps, 2 + taps, own)
        turns = first(jnp.stack([value[:, : 4 * width] for value in hops]))
        turns_came = swap(turns, (2, 4))
        pieces = second(turns, turns_came)
        cores = (rep & 1, 1 - (rep & 1))
        came = swap(pieces, (4, 2))
        pieces += [flip(value, 1) for value in pieces]
        left, right = place_weights(left, right, pieces, cores, True, rep, grp)
        pieces = [after(value, left) for value in came]
        ups = [after(value, *pieces) for value in ups]
        up_came = swap(ups, (4, 2))
        pieces += [flip(value, 1) for value in pieces]
        left, right = place_weights(left, right, pieces, cores, False, rep, grp)
        w_down = lax.all_gather(after(down_piece, pair_piece), "grp", axis=0, tiled=True)
    else:
        w_pair = lax.all_gather(pair_piece, "grp", axis=0, tiled=True)
        w_down = lax.all_gather(down_piece, "grp", axis=0, tiled=True)
        whole = lax.all_gather(sent, ("grp", "rep"), axis=0, tiled=True)
        left, right = whole[:, : 2 * width], whole[:, 2 * width :]
        small = lax.all_gather(gains, "grp", axis=0)
        ups_same = chips_gather(cotangent)
    small = small.swapaxes(0, 1).reshape(2 + taps, width).astype(F32)
    gain_one, gain_two, taps_f = small[0], small[1], small[2:]

    h_low, scale_one, b_part, c_part, x_part, edge = in_forward(tokens, gain_one[None], left, right)
    earlier = from_behind(edge[edge.shape[0] - (taps - 1) :], "grp", 1)
    gated, conv, z_low, resid, normed_two, scale_two, h2_low = out_forward(
        tokens,
        gain_two[None],
        taps_f,
        earlier,
        b_part,
        c_part,
        x_part,
        right,
    )
    w_x, w_out = right[:, :width], right[:, width:]

    flat = lambda value: value.reshape(chips * half, width)
    h2_last = h2_low[half:]
    if fast:
        parts = first(h2_low[:half])
        came = swap(parts, (2, 4))
        ups_same = third(ups, [after(value, *parts) for value in up_came])
        parts = second(parts, [after(value, w_pair, ups_same) for value in came])
        came = swap(parts, (4, 2))
        same = flat(third(parts, came))
        h2_last = after(h2_last, *came)
    else:
        same = flat(chips_gather(h2_low[:half]))
    h2_first = [same, flip(after(same, w_down) if fast else same, 1)]
    h2_last = [rep_gather(h2_last).reshape(reps * half, width)]
    if lanes > units:
        w_down = jnp.concatenate([w_down, jnp.zeros((lanes - units, width), BF16)], axis=0)

    ups_all = [ups_same, flip(ups_same, 1)]
    core = (rep & 1).reshape(1)
    acts0, boths0, second0, mixed = ffn(h2_first, ups_all, w_pair, w_down, core, 0)
    h2_last[0] = after(h2_last[0], second0)
    acts1, boths1, second1, mixed = ffn(h2_last, ups_all, w_pair, w_down, core, 1, [mixed])
    second0, second1 = rep_scatter(second0), rep_scatter(second1)
    down_grad = grad([after(acts0, mixed), acts1], ups_all * 2, (0, 0, 1, 1))
    down_sends = sends(down_grad[:units].reshape(grps, padded, width)[:, :piece])
    pair_grad = grad(
        [after(h2_first[0], second0, *down_sends), h2_first[1]] + h2_last, [boths0, boths1]
    )
    mixed = rep_scatter(mixed.reshape(reps * rows, width))
    pair_sends = sends(pair_grad.reshape(grps, own, 2 * lanes))
    if fast:
        down_turns = turned(down_sends)
        down_turns[1] = after(down_turns[1], *pair_sends)
        second1, *down_turns = lax.optimization_barrier((second1, *down_turns))
    else:
        down_own = total(turned(down_sends)).astype(BF16)
        pair_own = total(turned(pair_sends)).astype(BF16)

    block = 4 * width // reps
    split = width // block
    if fast:
        d_resid, d_branch, d_c, d_conv, local_mid = mid_backward(
            second0, second1, cotangent, normed_two, scale_two, gain_two[None], right, conv, c_part
        )
        local_mid = local_mid[0]
        later = from_behind(d_conv[: taps - 1], "grp", -1)
        near = [turn(after(pair_sends[k], later), k) for k in (1, 3)]
        down_turns[0] = after(down_turns[0], d_conv)
        down_own = total(down_turns).astype(BF16)
        gated = after(gated, down_own)
        d_all, local_taps = taps_backward(
            d_conv, later, taps_f, b_part, x_part, gated, earlier, d_c, d_branch, block
        )
        local_taps = list(local_taps)
    else:
        d_second = jnp.concatenate([second0, second1], axis=0).astype(F32)
        local_mid = jnp.sum(d_second * normed_two, axis=0)
        d_normed_two = d_second * gain_two
        d_resid = cotangent.astype(F32) + scale_two * (
            d_normed_two - normed_two * jnp.mean(d_normed_two * normed_two, axis=-1, keepdims=True)
        )
        d_branch = d_resid.astype(BF16)
        d_z = right_transposed(d_branch, w_out)
        d_c = d_z * conv
        d_conv = d_z * c_part
        later = from_behind(d_conv[: taps - 1], "grp", -1)
        padded_back = jnp.concatenate([d_conv, later], axis=0)
        d_gated = taps_f[0] * padded_back[taps - 1 : taps - 1 + rows]
        for tap in range(1, taps):
            ahead = taps - 1 - tap
            d_gated = d_gated + taps_f[tap] * padded_back[ahead : ahead + rows]
        before_it = jnp.concatenate([earlier, gated], axis=0)
        local_taps = [jnp.sum(d_conv * before_it[tap : tap + rows], axis=0) for tap in range(taps)]
        d_all = jnp.concatenate([d_gated * x_part, d_c, d_gated * b_part], axis=1).astype(BF16)
        d_all = jnp.concatenate([d_all, d_branch], axis=1)
        d_all = d_all.reshape(rows, reps, block).swapaxes(0, 1)

    lefts = jnp.stack([h_low, z_low])
    if fast:
        places = lambda *ms: jnp.stack([rep ^ m for m in ms])
        grads_one = block_grads(places(7, 3), lefts, d_all)
        flips_one = [flip(value, 1) for value in grads_one]
        grads_two = block_grads(places(5, 1), lefts, after(d_all, *grads_one))
        flips_two = [flip(value, 1) for value in grads_two]
        d_all = after(d_all, *grads_two)
        up6, low6, up2, low2 = block_grads(
            places(6, 2), lefts, d_all, flips_one, (BF16, BF16, BF16, F32)
        )
        ones = flip(jnp.stack([up6, up2]), 2)
        d_all = after(d_all, up6)
        up4, low4, up0, low0 = block_grads(
            places(4, 0), lefts, d_all, flips_two, (F32, BF16, F32, F32)
        )
        twos = flip(jnp.stack([low6, low4]), 4)
        d_all = after(d_all, up4, down_own)
    else:
        summed = jnp.concatenate(
            [
                left_product(h_low if j < 3 * split else z_low, d_all[j]).astype(BF16)
                for j in range(reps)
            ]
        )
        summed = lax.psum_scatter(summed, "rep", scatter_dimension=0, tiled=True)

    d_left = jnp.concatenate([d_all[j] for j in range(2 * split)], axis=1)
    d_right = jnp.concatenate([d_all[2 * split + j] for j in range(split)], axis=1)
    d_hidden = right_transposed(d_left, left) + right_transposed(d_right, w_x)
    normed = tokens.astype(F32) * scale_one
    local_in = jnp.sum(d_hidden * normed, axis=0)
    d_normed = d_hidden * gain_one
    input_grad = d_resid + scale_one * (
        d_normed - normed * jnp.mean(d_normed * normed, axis=-1, keepdims=True)
    )
    sums = jnp.stack([local_in, local_mid] + local_taps)
    if fast:
        far_gate = turn(after(pair_sends[2][:, :lanes], d_left), 2)
        ones, twos, mixed, near[0], near[1], far_gate, _ = lax.optimization_barrier(
            (ones, twos, mixed, near[0], near[1], far_gate, input_grad)
        )
        one6, one2, two6, two4 = ones[0], ones[1], twos[0], twos[1]
        one4_send = (up4 + one6.astype(F32)).astype(BF16)
        two2_send = (low2 + two6.astype(F32)).astype(BF16)
        one4, two2 = flip(one4_send, 4), flip(two2_send, 2)
        far_up = turn(after(pair_sends[2][:, lanes:], one4_send, two2_send), 2)
        sums = after(sums, one4_send, two2_send)
        sums = sums + flip(sums, 1)
        sums_came = swap([sums] * 3, (2, 4, 6))
        sums = (sums + sums_came[0]) + (sums_came[1] + sums_came[2])
        one4, two2, far_up, sums = lax.optimization_barrier((one4, two2, far_up, sums))
        far = jnp.concatenate([far_gate, far_up], axis=1)
        pair_own = total([pair_sends[0], near[0], far, near[1]]).astype(BF16)
        one2, two4 = after(one2, pair_own), after(two4, pair_own)
        one0 = up0 + one2.astype(F32) + one4.astype(F32)
        two0 = low0 + two4.astype(F32) + two2.astype(F32)
        summed = jnp.concatenate([one0, two0], axis=0).astype(BF16)
        sums = sums.reshape(2 + taps, grps, own).swapaxes(0, 1)
        high = lax.reduce_precision(sums, 8, 7)
        sums = jnp.stack([high.astype(BF16), (sums - high).astype(BF16)], axis=1)
        sums = sums.reshape(grps, -1, block)
        sum_rows = sums.shape[1]
        sums = jnp.pad(sums, ((0, 0), (0, -sum_rows % 16), (0, 0)))
        conv_sends = sends(jnp.concatenate([summed.reshape(grps, own, block), sums], axis=1))
        conv_near = [turn(conv_sends[k], k) for k in (1, 3)]
        conv_far = turn(conv_sends[2], 2)
        conv_turns = [conv_sends[0], conv_near[0], conv_far, conv_near[1]]
    else:
        sums = lax.psum(sums, "rep").reshape(2 + taps, grps, own).swapaxes(0, 1)
        owned = total(turned(sends(sums)))
        conv_turns = turned(sends(summed.reshape(grps, own, block)))
    down_full = rep_gather(down_own).reshape(-1, width)
    if fast:
        down_full = after(down_full, *conv_near)
    down_full = down_full.astype(F32)
    pair_full = rep_gather(pair_own)
    mixed = mixed.astype(F32)
    if fast:
        mixed = after(mixed, *conv_near)
    mixed = (resid + mixed).astype(BF16)
    if fast:
        conv_turns[1] = after(conv_turns[1], mixed, down_full)
        conv_own = total(conv_turns)
        owned = conv_own[own : own + sum_rows].reshape(2, 2 + taps, own).sum(axis=0)
        parts = first(conv_own[:own].astype(BF16))
        came = swap(parts, (2, 4))
        parts = second(parts, came)
        came = swap(parts, (4, 2))
        gate_full, up_full = spread(pair_full, grps, piece, padded)
        conv_same = third(parts, [after(value, gate_full, up_full) for value in came])
    else:
        conv_same = chips_gather(total(conv_turns).astype(BF16))
        gate_full, up_full = spread(pair_full, grps, piece, padded)
    conv_other = flip(conv_same, 1)
    in_full, out_full = unblock((rep & 1).reshape(1), conv_same, conv_other, width)
    return (
        mixed,
        input_grad,
        owned[0],
        in_full,
        owned[2:].T,
        out_full,
        owned[1],
        gate_full,
        up_full,
        down_full,
    )


def solution(mesh):
    placed = (
        P(("rep", "grp"), None),
        P("grp"),
        P("grp", None),
        P("grp", None),
        P("grp", None),
        P("grp"),
        P("grp", None),
        P("grp", None),
        P("grp", None),
        P(("rep", "grp"), None),
    )
    return jax.shard_map(
        shards,
        mesh=mesh,
        in_specs=placed,
        out_specs=(
            P(("rep", "grp"), None),
            P(("rep", "grp"), None),
            P("grp"),
            P("grp", None),
            P("grp", None),
            P("grp", None),
            P("grp"),
            P("grp", None),
            P("grp", None),
            P("grp", None),
        ),
        check_vma=False,
    )
```

```python
import functools

import jax
import jax.numpy as jnp
from jax import lax
from jax.experimental import pallas as pl
from jax.experimental.pallas import tpu as pltpu
from jax.sharding import PartitionSpec as P

EPS = 1e-05
F32, BF16 = jnp.float32, jnp.bfloat16
LIGHT = pl.CostEstimate(flops=1, bytes_accessed=1, transcendentals=0)


def after(value, *others):
    return lax.optimization_barrier((value,) + others)[0]


def from_behind(value, axis, steps):
    count = lax.axis_size(axis)
    first, last = (max(0, -steps), min(count, count - steps))
    return lax.ppermute(value, axis, [(source, source + steps) for source in range(first, last)])


def product(left, right):
    return jnp.dot(left, right, preferred_element_type=F32)


def left_product(left, right):
    return lax.dot_general(left, right, (((0,), (0,)), ((), ())), preferred_element_type=F32)


def right_transposed(left, right):
    return lax.dot_general(left, right, (((1,), (1,)), ((), ())), preferred_element_type=F32)


def turn(value, places):
    count = lax.axis_size("grp")
    return lax.ppermute(value, "grp", [(i, (i + places) % count) for i in range(count)])


def behind(places):
    count = lax.axis_size("grp")
    return lax.rem(lax.axis_index("grp") - places + count, count)


def placed(values):
    out = jnp.zeros((len(values),) + values[0].shape, values[0].dtype)
    for places, value in enumerate(values):
        out = lax.dynamic_update_index_in_dim(out, value, behind(places), 0)
    return out


def sends(parts):
    return [
        lax.dynamic_index_in_dim(parts, behind(-places), 0, keepdims=False)
        for places in range(lax.axis_size("grp"))
    ]


def turned(parts):
    return parts[:1] + [turn(part, places + 1) for places, part in enumerate(parts[1:])]


def total(parts):
    return sum(part.astype(F32) for part in parts)


def flip(value, bit):
    return lax.ppermute(value, "rep", [(i, i ^ bit) for i in range(lax.axis_size("rep"))])


def pair(mine, other, bit, axis):
    low = (lax.axis_index("rep") & bit) == 0
    return jnp.stack([jnp.where(low, mine, other), jnp.where(low, other, mine)], axis)


def same_core():
    chips = lax.axis_size("rep") // 2
    return [[2 * chip + core for chip in range(chips)] for core in range(2)]


def chips_gather(value):
    return lax.all_gather(value, "rep", axis=0, axis_index_groups=same_core())


def chips_gather_two(one, two):
    if lax.axis_size("rep") != 8:
        return chips_gather(one), chips_gather(two)
    one_x, two_y = flip(one, 2), flip(two, 4)
    one, two = pair(one, one_x, 2, 0), pair(two, two_y, 4, 0)
    one_y, two_x = flip(one, 4), flip(two, 2)
    one, two = pair(one, one_y, 4, 0), pair(two, two_x, 2, 1)
    return one.reshape((4,) + one.shape[2:]), two.reshape((4,) + two.shape[2:])


def chips_gather_steps(value):
    half = value.shape[-1] // 2
    return jnp.concatenate(chips_gather_two(value[..., :half], value[..., half:]), axis=-1)


def chips_scatter(value):
    return lax.psum_scatter(
        value, "rep", scatter_dimension=0, tiled=True, axis_index_groups=same_core()
    )


def chips_scatter_steps(value):
    if lax.axis_size("rep") != 8:
        return chips_scatter(value).astype(F32)
    rep = lax.axis_index("rep")
    rows, half = value.shape[0] // 4, value.shape[1] // 2

    def split(part, bit, axis):
        mine = jnp.where((rep & bit) == 0, 0, 1)
        pick = lambda i: lax.dynamic_index_in_dim(part, i, axis, keepdims=False)
        return pick(mine).astype(F32), pick(1 - mine).astype(BF16)

    value = value.reshape(2, 2, rows, 2 * half)
    one, send_one = split(value[..., :half], 2, 1)
    two, send_two = split(value[..., half:], 4, 0)
    one, two = one + flip(send_one, 2).astype(F32), two + flip(send_two, 4).astype(F32)
    one, send_one = split(one, 4, 0)
    two, send_two = split(two, 2, 0)
    one, two = one + flip(send_one, 4).astype(F32), two + flip(send_two, 2).astype(F32)
    return jnp.concatenate([one, two], axis=-1)


def rep_scatter(value):
    return lax.psum_scatter(value, "rep", scatter_dimension=0, tiled=True)


def rep_gather(value):
    return lax.all_gather(value, "rep", axis=0)


def spread_kernel(piece, padded, groups, pair_ref, gate_ref, up_ref):
    reps, _, lanes = pair_ref.shape
    for start, out_ref in ((0, gate_ref), (lanes // 2, up_ref)):
        for j in range(groups):
            for rep in range(reps):
                place, source = (j * reps + rep) * piece, start + j * padded
                out_ref[:, place : place + piece] = pair_ref[
                    rep, :, source : source + piece
                ].astype(F32)


def spread(part, groups, piece, padded):
    reps, rows, lanes = part.shape
    hidden = reps * groups * piece
    tile = 64
    return pl.pallas_call(
        functools.partial(spread_kernel, piece, padded, groups),
        grid=(rows // tile,),
        in_specs=[pl.BlockSpec((reps, tile, lanes), lambda i: (0, i, 0))],
        out_specs=[pl.BlockSpec((tile, hidden), lambda i: (i, 0))] * 2,
        out_shape=[jax.ShapeDtypeStruct((rows, hidden), F32)] * 2,
        compiler_params=pltpu.CompilerParams(vmem_limit_bytes=60 * 2**20),
        cost_estimate=pl.CostEstimate(flops=0, bytes_accessed=rows * hidden * 12, transcendentals=0),
    )(part)


def place_kernel(count, steps, table_ref, *refs):
    del table_ref
    step = pl.program_id(0)
    left_ref, right_ref = refs[-2:]
    for k in range(count):

        @pl.when((step >= k * steps) & (step < (k + 1) * steps))
        def _(k=k):
            left_ref[...] = refs[2 * k][0, 0]
            right_ref[...] = refs[2 * k + 1][0, 0]


def place_weights(left, right, pieces, cores, near, rep, grp):
    _, turns, cut, cols = pieces[0].shape
    own = left.shape[0] // (turns + 1)
    x, y = (rep >> 1) & 1, rep >> 2
    if not near:
        x, y = 1 - x, 1 - y
    rows = lambda places, chip, core: behind(places) * (own // cut) + 2 * chip + core
    table = jnp.stack(
        [
            rows(places, chip, core)
            for which in range(2)
            for core in cores
            for line in range(2)
            for places in range(1, turns + 1)
            for chip in ((2 * y + line, 2 * line + x)[which],)
        ]
    )
    count, steps = len(cores), 2 * turns

    def came(k):
        def index(i, table):
            step = jnp.clip(i - k * steps, 0, steps - 1)
            return (step // turns, step % turns, 0, 0)

        return pl.BlockSpec((1, 1, cut, cols), index)

    anywhere = pl.BlockSpec(memory_space=pl.ANY)
    total_steps = count * steps
    return pl.pallas_call(
        lambda table_ref, *refs: place_kernel(count, steps, table_ref, *refs[2:]),
        grid_spec=pltpu.PrefetchScalarGridSpec(
            num_scalar_prefetch=1,
            grid=(total_steps,),
            in_specs=[anywhere] * 2 + [came(k // 2) for k in range(2 * count)],
            out_specs=[
                pl.BlockSpec((cut, cols), lambda i, table: (table[i], 0)),
                pl.BlockSpec((cut, cols), lambda i, table: (table[total_steps + i], 0)),
            ],
        ),
        out_shape=[jax.ShapeDtypeStruct(left.shape, BF16)] * 2,
        input_output_aliases={1: 0, 2: 1},
        compiler_params=pltpu.CompilerParams(vmem_limit_bytes=60 * 2**20),
        cost_estimate=LIGHT,
    )(table, left, right, *pieces)


def in_kernel(tokens_ref, gain_ref, b_ref, c_ref, x_ref, h_ref, scale_ref, b_out, c_out, x_out, edge_ref):
    @pl.when(pl.program_id(0) == 0)
    def _():
        inputs = tokens_ref[...].astype(F32)
        scale = lax.rsqrt(jnp.mean(inputs * inputs, axis=-1, keepdims=True) + EPS)
        scale_ref[...] = scale
        h_ref[...] = (inputs * scale * gain_ref[...]).astype(BF16)

    h_low = h_ref[...]
    b_part = product(h_low, b_ref[...])
    x_part = product(h_low, x_ref[...])
    b_out[...] = b_part
    x_out[...] = x_part
    c_out[...] = product(h_low, c_ref[...])
    edge_ref[...] = (b_part * x_part)[-edge_ref.shape[0] :]


def in_forward(tokens, gain, left, right):
    rows, width = tokens.shape
    cols = 256
    count = width // cols
    whole = pl.BlockSpec((rows, width), lambda i: (0, 0))
    column = pl.BlockSpec((rows, cols), lambda i: (0, i))
    weight = lambda start: pl.BlockSpec((width, cols), lambda i: (0, start + i))
    part = jax.ShapeDtypeStruct((rows, width), F32)
    return pl.pallas_call(
        in_kernel,
        grid=(count,),
        in_specs=[
            whole,
            pl.BlockSpec((1, width), lambda i: (0, 0)),
            weight(0),
            weight(count),
            weight(0),
        ],
        out_specs=[
            whole,
            pl.BlockSpec((rows, 1), lambda i: (0, 0)),
            column,
            column,
            column,
            pl.BlockSpec((8, cols), lambda i: (0, i)),
        ],
        out_shape=[
            jax.ShapeDtypeStruct((rows, width), BF16),
            jax.ShapeDtypeStruct((rows, 1), F32),
            part,
            part,
            part,
            jax.ShapeDtypeStruct((8, width), F32),
        ],
        compiler_params=pltpu.CompilerParams(vmem_limit_bytes=60 * 2**20),
        cost_estimate=LIGHT,
    )(tokens, gain, left, left, right)


def out_kernel(
    tokens_ref, gain_ref, taps_ref, earlier_ref, b_ref, c_ref, x_ref, w_ref,
    gated_ref, conv_ref, z_ref, resid_ref, normed_ref, scale_ref, h2_ref, sum_ref,
):
    step = pl.program_id(0)
    rows = b_ref.shape[0]
    gated = b_ref[...] * x_ref[...]
    gated_ref[...] = gated
    padded = jnp.concatenate([earlier_ref[...], gated], axis=0)
    conv = taps_ref[0:1] * padded[0:rows]
    for tap in range(1, taps_ref.shape[0]):
        conv = conv + taps_ref[tap : tap + 1] * padded[tap : tap + rows]
    conv_ref[...] = conv
    z_low = (c_ref[...] * conv).astype(BF16)
    z_ref[...] = z_low

    @pl.when(step == 0)
    def _():
        sum_ref[...] = tokens_ref[...].astype(F32)

    sum_ref[...] += product(z_low, w_ref[...])

    @pl.when(step == pl.num_programs(0) - 1)
    def _():
        resid = sum_ref[...]
        resid_ref[...] = resid
        scale = lax.rsqrt(jnp.mean(resid * resid, axis=-1, keepdims=True) + EPS)
        scale_ref[...] = scale
        normed = resid * scale
        normed_ref[...] = normed
        h2_ref[...] = (normed * gain_ref[...]).astype(BF16)


def out_forward(tokens, gain, taps_f, earlier, b_part, c_part, x_part, right):
    rows, width = tokens.shape
    cols = 256
    whole = pl.BlockSpec((rows, width), lambda i: (0, 0))
    column = lambda n: pl.BlockSpec((n, cols), lambda i: (0, i))
    full = lambda kind: jax.ShapeDtypeStruct((rows, width), kind)
    return pl.pallas_call(
        out_kernel,
        grid=(width // cols,),
        in_specs=[
            whole,
            pl.BlockSpec((1, width), lambda i: (0, 0)),
            column(taps_f.shape[0]),
            column(earlier.shape[0]),
            column(rows),
            column(rows),
            column(rows),
            pl.BlockSpec((cols, width), lambda i: (i, 1)),
        ],
        out_specs=[
            column(rows),
            column(rows),
            column(rows),
            whole,
            whole,
            pl.BlockSpec((rows, 1), lambda i: (0, 0)),
            whole,
        ],
        out_shape=[
            full(F32),
            full(F32),
            full(BF16),
            full(F32),
            full(F32),
            jax.ShapeDtypeStruct((rows, 1), F32),
            full(BF16),
        ],
        scratch_shapes=[pltpu.VMEM((rows, width), F32)],
        compiler_params=pltpu.CompilerParams(vmem_limit_bytes=60 * 2**20),
        cost_estimate=LIGHT,
    )(tokens, gain, taps_f, earlier, b_part, c_part, x_part, right)


def mid_kernel(
    second0_ref, second1_ref, up_ref, normed_ref, scale_ref, gain_ref, w_ref, conv_ref, c_ref,
    resid_ref, branch_ref, d_c_ref, d_conv_ref, sum_ref,
):
    step, half_steps = pl.program_id(0), pl.num_programs(0) // 2

    @pl.when(step == 0)
    def _():
        sum_ref[...] = jnp.zeros_like(sum_ref)

    d_second = jnp.where(step < half_steps, second0_ref[...], second1_ref[...]).astype(F32)
    normed = normed_ref[...]
    both = d_second * normed
    sum_ref[...] += jnp.sum(both, axis=0, keepdims=True)
    d_normed = d_second * gain_ref[...]
    mean = jnp.mean(d_normed * normed, axis=-1, keepdims=True)
    d_resid = up_ref[...].astype(F32) + scale_ref[...] * (d_normed - normed * mean)
    resid_ref[...] = d_resid
    branch = d_resid.astype(BF16)
    branch_ref[...] = branch
    d_z = right_transposed(branch, w_ref[...])
    d_c_ref[...] = (d_z * conv_ref[...]).astype(BF16)
    d_conv_ref[...] = d_z * c_ref[...]


def mid_backward(second0, second1, upstream, normed, scale, gain, right, conv, c_part):
    rows, width = normed.shape
    tile = rows // 2
    steps = 2
    row = pl.BlockSpec((tile, width), lambda i: (i, 0))
    first = pl.BlockSpec((tile, width), lambda i: (jnp.minimum(i, steps // 2 - 1), 0))
    last = pl.BlockSpec((tile, width), lambda i: (jnp.maximum(i - steps // 2, 0), 0))
    line = pl.BlockSpec((1, width), lambda i: (0, 0))
    return pl.pallas_call(
        mid_kernel,
        grid=(steps,),
        in_specs=[
            first,
            last,
            row,
            row,
            pl.BlockSpec((tile, 1), lambda i: (i, 0)),
            line,
            pl.BlockSpec((width, width), lambda i: (0, 1)),
            row,
            row,
        ],
        out_specs=[row, row, row, row, line],
        out_shape=[
            jax.ShapeDtypeStruct((rows, width), F32),
            jax.ShapeDtypeStruct((rows, width), BF16),
            jax.ShapeDtypeStruct((rows, width), BF16),
            jax.ShapeDtypeStruct((rows, width), F32),
            jax.ShapeDtypeStruct((1, width), F32),
        ],
        compiler_params=pltpu.CompilerParams(vmem_limit_bytes=60 * 2**20),
        cost_estimate=LIGHT,
    )(second0, second1, upstream, normed, scale, gain, right, conv, c_part)


def taps_kernel(d_conv_ref, later_ref, taps_ref, b_ref, x_ref, u_ref, earlier_ref, d_c_ref, branch_ref, all_ref, sum_ref):
    rows = d_conv_ref.shape[0]
    taps = taps_ref.shape[0]
    d_conv = d_conv_ref[...]
    after_it = jnp.concatenate([d_conv, later_ref[...]], axis=0)
    before_it = jnp.concatenate([earlier_ref[...], u_ref[...]], axis=0)
    d_gated = jnp.zeros_like(d_conv)
    for tap in range(taps):
        ahead = taps - 1 - tap
        d_gated = d_gated + taps_ref[tap : tap + 1] * after_it[ahead : ahead + rows]
        sum_ref[tap : tap + 1] = jnp.sum(d_conv * before_it[tap : tap + rows], axis=0, keepdims=True)
    all_ref[0, 0] = (d_gated * x_ref[...]).astype(BF16)
    all_ref[1, 0] = d_c_ref[...]
    all_ref[2, 0] = (d_gated * b_ref[...]).astype(BF16)
    all_ref[3, 0] = branch_ref[...]


def taps_backward(d_conv, later, taps_f, b_part, x_part, gated, earlier, d_c, branch, block):
    rows, width = d_conv.shape
    taps = taps_f.shape[0]
    cols = 256
    per = block // cols
    column = lambda n: pl.BlockSpec((n, cols), lambda i: (0, i))
    d_all, sums = pl.pallas_call(
        taps_kernel,
        grid=(width // cols,),
        in_specs=[
            column(rows),
            column(taps - 1),
            column(taps),
            column(rows),
            column(rows),
            column(rows),
            column(taps - 1),
            column(rows),
            column(rows),
        ],
        out_specs=[
            pl.BlockSpec((4, 1, rows, cols), lambda i: (0, i // per, 0, i % per)),
            column(taps),
        ],
        out_shape=[
            jax.ShapeDtypeStruct((4, width // block, rows, block), BF16),
            jax.ShapeDtypeStruct((taps, width), F32),
        ],
        compiler_params=pltpu.CompilerParams(vmem_limit_bytes=60 * 2**20),
        cost_estimate=LIGHT,
    )(d_conv, later, taps_f, b_part, x_part, gated, earlier, d_c, branch)
    return d_all.reshape(-1, rows, block), sums


def ffn_kernel(core_ref, same_ref, other_ref, up_same_ref, up_other_ref, pair_ref, down_ref, *refs):
    del core_ref
    act_ref, both_ref, second_ref, mixed_ref = refs[-4:]
    lanes, width = down_ref.shape
    first_half = pl.program_id(0) < pl.num_programs(0) // 2
    rows = lambda ref: ref[...].reshape(-1, width)
    h2 = jnp.where(first_half, rows(same_ref), rows(other_ref))
    up_g = jnp.where(first_half, rows(up_same_ref), rows(up_other_ref))
    both = product(h2, pair_ref[...])
    gate, upper = both[:, :lanes], both[:, lanes:]
    sigma = jax.nn.sigmoid(gate)
    swish = gate * sigma
    act = (swish * upper).astype(BF16)
    act_ref[...] = act
    d_act = right_transposed(up_g, down_ref[...])
    d_gate = (d_act * upper * sigma * (1.0 + gate * (1.0 - sigma))).astype(BF16)
    d_upper = (d_act * swish).astype(BF16)
    both_ref[...] = jnp.concatenate([d_gate, d_upper], axis=1).reshape(both_ref.shape)
    second = right_transposed(both_ref[...].reshape(-1, 2 * lanes), pair_ref[...]).astype(BF16)
    second_ref[...] = second.reshape(second_ref.shape)
    mixed_ref[...] = product(act, down_ref[...]).astype(BF16).reshape(mixed_ref.shape)


def ffn(h2s, ups, w_pair, w_down, core, which, filled=()):
    chips, tile, width = ups[0].shape
    tile //= 2
    lanes = w_down.shape[0]
    natural = len(h2s) == 1
    per = 2
    steps = chips // per
    turns = [lambda i: jnp.minimum(i, steps - 1), lambda i: jnp.maximum(i - steps, 0)]
    side = lambda i, core: jnp.where(i < steps, core[0], 1 - core[0])
    plain = lambda n: pl.BlockSpec((per * tile, n), lambda i, core: (i, 0))
    ordered = lambda n: pl.BlockSpec(
        (per, 1, tile, n), lambda i, core: (i % steps, side(i, core), 0, 0)
    )
    full = lambda w: pl.BlockSpec(w.shape, lambda i, core: (0, 0), pipeline_mode=pl.Buffered(1))
    if natural:
        h2s = [h2s[0].reshape(chips, 2, tile, width)] * 2
        h2_specs = [
            pl.BlockSpec((per, 1, tile, width), lambda i, core, k=k: (turns[k](i), core[0] ^ k, 0, 0))
            for k in range(2)
        ]
    else:
        h2s = [value.reshape(chips, tile, width) for value in h2s]
        h2_specs = [
            pl.BlockSpec((per, tile, width), lambda i, core, k=k: (turns[k](i), 0, 0))
            for k in range(2)
        ]
    tokens = 2 * chips * tile
    placed_ = lambda n: jax.ShapeDtypeStruct((chips, 2, tile, n), BF16)
    acts, boths, second, mixed = pl.pallas_call(
        ffn_kernel,
        grid_spec=pltpu.PrefetchScalarGridSpec(
            num_scalar_prefetch=1,
            grid=(2 * steps,),
            in_specs=h2_specs
            + [
                pl.BlockSpec((per, tile, width), lambda i, core, at=at: (at(i), which, 0))
                for at in turns
            ]
            + [full(w_pair), full(w_down)]
            + [pl.BlockSpec(memory_space=pl.ANY) for _ in filled],
            out_specs=[
                plain(lanes),
                ordered(2 * lanes) if natural else plain(2 * lanes),
                ordered(width),
                pl.BlockSpec(
                    (per, 1, 1, tile, width),
                    lambda i, core: (i % steps, side(i, core), which, 0, 0),
                ),
            ],
        ),
        out_shape=[
            jax.ShapeDtypeStruct((tokens, lanes), BF16),
            placed_(2 * lanes) if natural else jax.ShapeDtypeStruct((tokens, 2 * lanes), BF16),
            placed_(width),
            jax.ShapeDtypeStruct((chips, 2, 2, tile, width), BF16),
        ],
        input_output_aliases={7: 3} if filled else {},
        compiler_params=pltpu.CompilerParams(vmem_limit_bytes=60 * 2**20),
        cost_estimate=pl.CostEstimate(
            flops=17 * tokens * width * lanes, bytes_accessed=0, transcendentals=0
        ),
    )(core, *h2s, *ups, w_pair, w_down, *filled)
    return acts, boths.reshape(tokens, -1), second.reshape(tokens, width), mixed


def grad_kernel(parts, lefts_count, *refs):
    lefts, rights, out_ref, total_ref = (
        refs[:lefts_count],
        refs[lefts_count:-2],
        refs[-2],
        refs[-1],
    )
    step = pl.program_id(0)

    @pl.when(step == 0)
    def _():
        total_ref[...] = jnp.zeros_like(total_ref)

    for start, stop, left, right in parts:

        @pl.when((step >= start) & (step < stop))
        def _(left=left, right=right):
            value = rights[right][...]
            value = value.reshape(-1, value.shape[-1])
            total_ref[...] += left_product(lefts[left][...], value)

    @pl.when(step == pl.num_programs(0) - 1)
    def _():
        out_ref[...] = total_ref[...].astype(BF16)


def grad(lefts, rights, halves=None):
    tile = 480
    n, m = lefts[0].shape[1], rights[0].shape[-1]

    def cuts(arrays):
        out = [0]
        for array in arrays:
            out.append(out[-1] + array.size // array.shape[-1] // tile // (array.ndim - 1))
        return out

    left_cuts, right_cuts = cuts(lefts), cuts(rights)
    edges = sorted(set(left_cuts + right_cuts))
    find = lambda which, step: max(k for k in range(len(which) - 1) if which[k] <= step)
    parts = [
        (start, stop, find(left_cuts, start), find(right_cuts, start))
        for start, stop in zip(edges, edges[1:])
    ]

    def spec(which, k, array):
        at = lambda i: jnp.clip(i, which[k], which[k + 1] - 1) - which[k]
        if array.ndim == 2:
            return pl.BlockSpec((tile, array.shape[1]), lambda i: (at(i), 0))
        half = array.shape[1] // 2
        return pl.BlockSpec((tile // half, half, array.shape[2]), lambda i: (at(i), halves[k], 0))

    return pl.pallas_call(
        functools.partial(grad_kernel, parts, len(lefts)),
        grid=(edges[-1],),
        in_specs=[spec(left_cuts, k, array) for k, array in enumerate(lefts)]
        + [spec(right_cuts, k, array) for k, array in enumerate(rights)],
        out_specs=pl.BlockSpec((n, m), lambda i: (0, 0)),
        out_shape=jax.ShapeDtypeStruct((n, m), BF16),
        scratch_shapes=[pltpu.VMEM((n, m), F32)],
        compiler_params=pltpu.CompilerParams(vmem_limit_bytes=60 * 2**20),
        cost_estimate=pl.CostEstimate(flops=3 * tile * edges[-1] * n * m, bytes_accessed=0, transcendentals=0),
    )(*lefts, *rights)


def block_kernel(count, kept, places_ref, *refs):
    del places_ref
    lefts, rights, refs = refs[:count], refs[count : 2 * count], refs[2 * count :]
    for k in range(count):
        total_ = left_product(lefts[k][0], rights[k][0])
        if not kept:
            refs[k][...] = total_.astype(BF16)
            continue
        total_ = total_ + refs[k][...].astype(F32)
        for which in range(2):

            @pl.when(pl.program_id(0) == which)
            def _(k=k, which=which, total_=total_):
                ref = refs[count + 2 * k + which]
                ref[...] = total_.astype(ref.dtype)


def block_grads(places, lefts, rights, came=(), kept=()):
    count = places.shape[0]
    rows, width = lefts.shape[1:]
    blocks, _, block = rights.shape
    branch = blocks - blocks // 4
    left = lambda k: pl.BlockSpec(
        (1, rows, width // 2), lambda i, places: ((places[k] >= branch).astype(jnp.int32), 0, i)
    )
    right = lambda k: pl.BlockSpec((1, rows, block), lambda i, places: (places[k], 0, 0))
    moving = pl.BlockSpec((width // 2, block), lambda i, places: (i, 0))
    fixed = pl.BlockSpec((width // 2, block), lambda i, places: (0, 0))
    if kept:
        outs = [jax.ShapeDtypeStruct((width // 2, block), kind) for kind in kept]
    else:
        outs = [jax.ShapeDtypeStruct((width, block), BF16)] * count
    return pl.pallas_call(
        functools.partial(block_kernel, count, bool(kept)),
        grid_spec=pltpu.PrefetchScalarGridSpec(
            num_scalar_prefetch=1,
            grid=(2,),
            in_specs=[left(k) for k in range(count)]
            + [right(k) for k in range(count)]
            + [moving for _ in came],
            out_specs=[fixed if kept else moving for _ in outs],
        ),
        out_shape=outs,
        compiler_params=pltpu.CompilerParams(vmem_limit_bytes=40 * 2**20),
        cost_estimate=LIGHT,
    )(places, *([lefts] * count), *([rights] * count), *came)


def unblock_kernel(core_ref, same_ref, other_ref, in_ref, out_ref):
    chips, _, block = same_ref.shape
    first = core_ref[0] == 0
    for chip in range(chips):
        same, other = same_ref[chip].astype(F32), other_ref[chip].astype(F32)
        for core, value in enumerate((jnp.where(first, same, other), jnp.where(first, other, same))):
            place = (2 * chip + core) * block
            if place < in_ref.shape[1]:
                in_ref[:, place : place + block] = value
            else:
                place -= in_ref.shape[1]
                out_ref[:, place : place + block] = value


def unblock(core, same, other, width):
    chips, rows, block = same.shape
    tile = 96
    spec = pl.BlockSpec((chips, tile, block), lambda i, core: (0, i, 0))
    return pl.pallas_call(
        unblock_kernel,
        grid_spec=pltpu.PrefetchScalarGridSpec(
            num_scalar_prefetch=1,
            grid=(rows // tile,),
            in_specs=[spec, spec],
            out_specs=[pl.BlockSpec((tile, n), lambda i, core: (i, 0)) for n in (3 * width, width)],
        ),
        out_shape=[jax.ShapeDtypeStruct((rows, n), F32) for n in (3 * width, width)],
        compiler_params=pltpu.CompilerParams(vmem_limit_bytes=60 * 2**20),
        cost_estimate=pl.CostEstimate(flops=0, bytes_accessed=24 * rows * width, transcendentals=0),
    )(core, same, other)


def shards(
    tokens,
    norm_in,
    in_weight,
    conv_weight,
    out_weight,
    norm_mid,
    gate_weight,
    up_weight,
    down_weight,
    cotangent,
):
    reps, grps = lax.axis_size("rep"), lax.axis_size("grp")
    rep, grp = lax.axis_index("rep"), lax.axis_index("grp")
    chips = reps // 2
    low_core = (rep & 1) == 0
    rows, width = tokens.shape
    taps = conv_weight.shape[1]
    own = in_weight.shape[0]
    hidden = gate_weight.shape[1]
    piece = hidden // (reps * grps)
    padded = -(-piece // 16) * 16
    units = padded * grps
    lanes = -(-units // 128) * 128
    half = rows // 2

    def columns(weight):
        gap, parts = jnp.zeros((own, padded - piece), BF16), []
        for j in range(grps):
            place = j * (hidden // grps) + rep * piece
            parts += [lax.dynamic_slice(weight, (0, place), (own, piece)), gap]
        return jnp.concatenate(parts + [jnp.zeros((own, lanes - units), BF16)], axis=1)

    pair_piece = jnp.concatenate([columns(gate_weight), columns(up_weight)], axis=1)
    down_piece = lax.dynamic_slice_in_dim(down_weight, rep * piece, piece, 0)
    down_piece = jnp.pad(down_piece, ((0, padded - piece), (0, 0)))
    cut = own // reps
    gains = jnp.concatenate([norm_in[None], norm_mid[None], conv_weight.T], axis=0)
    sent = jnp.concatenate(
        [
            lax.dynamic_slice_in_dim(in_weight, rep * cut, cut, 0),
            lax.dynamic_slice_in_dim(out_weight, rep * cut, cut, 0),
        ],
        axis=1,
    )
    fast = reps == 8 and grps == 4
    if fast:
        def first(value):
            half_cols = value.shape[-1] // 2
            return [value[..., :half_cols], value[..., half_cols:]]

        def swap(values, bits):
            return [flip(value, bit) for value, bit in zip(values, bits)]

        def second(values, came):
            return [pair(values[0], came[0], 2, 0), pair(values[1], came[1], 4, 0)]

        def third(values, came):
            both = [pair(values[0], came[0], 4, 0), pair(values[1], came[1], 2, 1)]
            return jnp.concatenate([value.reshape((4,) + value.shape[2:]) for value in both], axis=-1)

        side = -(-gains.size // (cut * 128)) * 128
        gains = jnp.pad(gains.reshape(-1), (0, cut * side - gains.size)).reshape(cut, side)
        sent = jnp.concatenate([sent, gains], axis=1)
        near = [turn(sent, 1), turn(sent, 3)]
        ups = first(cotangent)
        left = jnp.zeros((width, 2 * width), BF16)
        left = lax.dynamic_update_slice(left, in_weight[:, : 2 * width], (grp * own, 0))
        right = jnp.zeros((width, 2 * width), BF16)
        right = lax.dynamic_update_slice(right, in_weight[:, 2 * width :], (grp * own, 0))
        right = lax.dynamic_update_slice(right, out_weight, (grp * own, width))
        came = [after(value, pair_piece, left, right, *near) for value in swap(ups, (2, 4))]
        ups = second(ups, came)
        far = turn(after(sent, *near), 2)
        w_pair = lax.all_gather(after(pair_piece, far), "grp", axis=0, tiled=True)
        hops = [after(near[0], *ups), far, near[1]]
        small = placed([gains] + [value[:, 4 * width :] for value in hops])
        small = small.reshape(grps, -1)[:, : (2 + taps) * own].reshape(grps, 2 + taps, own)
        turns = first(jnp.stack([value[:, : 4 * width] for value in hops]))
        turns_came = swap(turns, (2, 4))
        pieces = second(turns, turns_came)
        cores = (rep & 1, 1 - (rep & 1))
        came = swap(pieces, (4, 2))
        pieces += [flip(value, 1) for value in pieces]
        left, right = place_weights(left, right, pieces, cores, True, rep, grp)
        pieces = [after(value, left) for value in came]
        ups = [after(value, *pieces) for value in ups]
        up_came = swap(ups, (4, 2))
        pieces += [flip(value, 1) for value in pieces]
        left, right = place_weights(left, right, pieces, cores, False, rep, grp)
        w_down = lax.all_gather(after(down_piece, pair_piece), "grp", axis=0, tiled=True)
    else:
        w_pair = lax.all_gather(pair_piece, "grp", axis=0, tiled=True)
        w_down = lax.all_gather(down_piece, "grp", axis=0, tiled=True)
        whole = lax.all_gather(sent, ("grp", "rep"), axis=0, tiled=True)
        left, right = whole[:, : 2 * width], whole[:, 2 * width :]
        small = lax.all_gather(gains, "grp", axis=0)
        ups_same = chips_gather(cotangent)
    small = small.swapaxes(0, 1).reshape(2 + taps, width).astype(F32)
    gain_one, gain_two, taps_f = small[0], small[1], small[2:]

    h_low, scale_one, b_part, c_part, x_part, edge = in_forward(tokens, gain_one[None], left, right)
    earlier = from_behind(edge[edge.shape[0] - (taps - 1) :], "grp", 1)
    gated, conv, z_low, resid, normed_two, scale_two, h2_low = out_forward(
        tokens,
        gain_two[None],
        taps_f,
        earlier,
        b_part,
        c_part,
        x_part,
        right,
    )
    w_x, w_out = right[:, :width], right[:, width:]

    flat = lambda value: value.reshape(chips * half, width)
    h2_last = h2_low[half:]
    if fast:
        parts = first(h2_low[:half])
        came = swap(parts, (2, 4))
        ups_same = third(ups, [after(value, *parts) for value in up_came])
        parts = second(parts, [after(value, w_pair, ups_same) for value in came])
        came = swap(parts, (4, 2))
        same = flat(third(parts, came))
        h2_last = after(h2_last, *came)
    else:
        same = flat(chips_gather(h2_low[:half]))
    h2_first = [same, flip(after(same, w_down) if fast else same, 1)]
    h2_last = [rep_gather(h2_last).reshape(reps * half, width)]
    if lanes > units:
        w_down = jnp.concatenate([w_down, jnp.zeros((lanes - units, width), BF16)], axis=0)

    ups_all = [ups_same, flip(ups_same, 1)]
    core = (rep & 1).reshape(1)
    acts0, boths0, second0, mixed = ffn(h2_first, ups_all, w_pair, w_down, core, 0)
    h2_last[0] = after(h2_last[0], second0)
    acts1, boths1, second1, mixed = ffn(h2_last, ups_all, w_pair, w_down, core, 1, [mixed])
    second0, second1 = rep_scatter(second0), rep_scatter(second1)
    down_grad = grad([after(acts0, mixed), acts1], ups_all * 2, (0, 0, 1, 1))
    down_sends = sends(down_grad[:units].reshape(grps, padded, width)[:, :piece])
    pair_grad = grad(
        [after(h2_first[0], second0, *down_sends), h2_first[1]] + h2_last, [boths0, boths1]
    )
    mixed = rep_scatter(mixed.reshape(reps * rows, width))
    pair_sends = sends(pair_grad.reshape(grps, own, 2 * lanes))
    if fast:
        down_turns = turned(down_sends)
        down_turns[1] = after(down_turns[1], *pair_sends)
        second1, *down_turns = lax.optimization_barrier((second1, *down_turns))
    else:
        down_own = total(turned(down_sends)).astype(BF16)
        pair_own = total(turned(pair_sends)).astype(BF16)

    block = 4 * width // reps
    split = width // block
    if fast:
        d_resid, d_branch, d_c, d_conv, local_mid = mid_backward(
            second0, second1, cotangent, normed_two, scale_two, gain_two[None], right, conv, c_part
        )
        local_mid = local_mid[0]
        later = from_behind(d_conv[: taps - 1], "grp", -1)
        near = [turn(after(pair_sends[k], later), k) for k in (1, 3)]
        down_turns[0] = after(down_turns[0], d_conv)
        down_own = total(down_turns).astype(BF16)
        gated = after(gated, down_own)
        d_all, local_taps = taps_backward(
            d_conv, later, taps_f, b_part, x_part, gated, earlier, d_c, d_branch, block
        )
        local_taps = list(local_taps)
    else:
        d_second = jnp.concatenate([second0, second1], axis=0).astype(F32)
        local_mid = jnp.sum(d_second * normed_two, axis=0)
        d_normed_two = d_second * gain_two
        d_resid = cotangent.astype(F32) + scale_two * (
            d_normed_two - normed_two * jnp.mean(d_normed_two * normed_two, axis=-1, keepdims=True)
        )
        d_branch = d_resid.astype(BF16)
        d_z = right_transposed(d_branch, w_out)
        d_c = d_z * conv
        d_conv = d_z * c_part
        later = from_behind(d_conv[: taps - 1], "grp", -1)
        padded_back = jnp.concatenate([d_conv, later], axis=0)
        d_gated = taps_f[0] * padded_back[taps - 1 : taps - 1 + rows]
        for tap in range(1, taps):
            ahead = taps - 1 - tap
            d_gated = d_gated + taps_f[tap] * padded_back[ahead : ahead + rows]
        before_it = jnp.concatenate([earlier, gated], axis=0)
        local_taps = [jnp.sum(d_conv * before_it[tap : tap + rows], axis=0) for tap in range(taps)]
        d_all = jnp.concatenate([d_gated * x_part, d_c, d_gated * b_part], axis=1).astype(BF16)
        d_all = jnp.concatenate([d_all, d_branch], axis=1)
        d_all = d_all.reshape(rows, reps, block).swapaxes(0, 1)

    lefts = jnp.stack([h_low, z_low])
    if fast:
        places = lambda *ms: jnp.stack([rep ^ m for m in ms])
        grads_one = block_grads(places(7, 3), lefts, d_all)
        flips_one = [flip(value, 1) for value in grads_one]
        grads_two = block_grads(places(5, 1), lefts, after(d_all, *grads_one))
        flips_two = [flip(value, 1) for value in grads_two]
        d_all = after(d_all, *grads_two)
        up6, low6, up2, low2 = block_grads(
            places(6, 2), lefts, d_all, flips_one, (BF16, BF16, BF16, F32)
        )
        ones = flip(jnp.stack([up6, up2]), 2)
        d_all = after(d_all, up6)
        up4, low4, up0, low0 = block_grads(
            places(4, 0), lefts, d_all, flips_two, (F32, BF16, F32, F32)
        )
        twos = flip(jnp.stack([low6, low4]), 4)
        d_all = after(d_all, up4, down_own)
    else:
        summed = jnp.concatenate(
            [
                left_product(h_low if j < 3 * split else z_low, d_all[j]).astype(BF16)
                for j in range(reps)
            ]
        )
        summed = lax.psum_scatter(summed, "rep", scatter_dimension=0, tiled=True)

    d_left = jnp.concatenate([d_all[j] for j in range(2 * split)], axis=1)
    d_right = jnp.concatenate([d_all[2 * split + j] for j in range(split)], axis=1)
    d_hidden = right_transposed(d_left, left) + right_transposed(d_right, w_x)
    normed = tokens.astype(F32) * scale_one
    local_in = jnp.sum(d_hidden * normed, axis=0)
    d_normed = d_hidden * gain_one
    input_grad = d_resid + scale_one * (
        d_normed - normed * jnp.mean(d_normed * normed, axis=-1, keepdims=True)
    )
    sums = jnp.stack([local_in, local_mid] + local_taps)
    if fast:
        far_gate = turn(after(pair_sends[2][:, :lanes], d_left), 2)
        ones, twos, mixed, near[0], near[1], far_gate, _ = lax.optimization_barrier(
            (ones, twos, mixed, near[0], near[1], far_gate, input_grad)
        )
        one6, one2, two6, two4 = ones[0], ones[1], twos[0], twos[1]
        one4_send = (up4 + one6.astype(F32)).astype(BF16)
        two2_send = (low2 + two6.astype(F32)).astype(BF16)
        one4, two2 = flip(one4_send, 4), flip(two2_send, 2)
        far_up = turn(after(pair_sends[2][:, lanes:], one4_send, two2_send), 2)
        sums = after(sums, one4_send, two2_send)
        sums = sums + flip(sums, 1)
        sums_came = swap([sums] * 3, (2, 4, 6))
        sums = (sums + sums_came[0]) + (sums_came[1] + sums_came[2])
        one4, two2, far_up, sums = lax.optimization_barrier((one4, two2, far_up, sums))
        far = jnp.concatenate([far_gate, far_up], axis=1)
        pair_own = total([pair_sends[0], near[0], far, near[1]]).astype(BF16)
        sums = after(sums, pair_own)
        one0 = up0 + one2.astype(F32) + one4.astype(F32)
        two0 = low0 + two4.astype(F32) + two2.astype(F32)
        summed = jnp.concatenate([one0, two0], axis=0).astype(BF16)
        sums = sums.reshape(2 + taps, grps, own).swapaxes(0, 1)
        high = lax.reduce_precision(sums, 8, 7)
        sums = jnp.stack([high.astype(BF16), (sums - high).astype(BF16)], axis=1)
        sums = sums.reshape(grps, -1, block)
        sum_rows = sums.shape[1]
        sums = jnp.pad(sums, ((0, 0), (0, -sum_rows % 16), (0, 0)))
        conv_sends = sends(jnp.concatenate([summed.reshape(grps, own, block), sums], axis=1))
        conv_near = [turn(conv_sends[k], k) for k in (1, 3)]
        conv_far = turn(conv_sends[2], 2)
        conv_turns = [conv_sends[0], conv_near[0], conv_far, conv_near[1]]
    else:
        sums = lax.psum(sums, "rep").reshape(2 + taps, grps, own).swapaxes(0, 1)
        owned = total(turned(sends(sums)))
        conv_turns = turned(sends(summed.reshape(grps, own, block)))
    down_full = rep_gather(down_own).reshape(-1, width)
    if fast:
        down_full = after(down_full, *conv_near)
    down_full = down_full.astype(F32)
    pair_full = rep_gather(pair_own)
    mixed = mixed.astype(F32)
    if fast:
        mixed = after(mixed, *conv_near)
    mixed = (resid + mixed).astype(BF16)
    if fast:
        conv_turns[1] = after(conv_turns[1], mixed, down_full)
        conv_own = total(conv_turns)
        owned = conv_own[own : own + sum_rows].reshape(2, 2 + taps, own).sum(axis=0)
        parts = first(conv_own[:own].astype(BF16))
        came = swap(parts, (2, 4))
        parts = second(parts, came)
        came = swap(parts, (4, 2))
        gate_full, up_full = spread(pair_full, grps, piece, padded)
        conv_same = third(parts, [after(value, gate_full, up_full) for value in came])
    else:
        conv_same = chips_gather(total(conv_turns).astype(BF16))
        gate_full, up_full = spread(pair_full, grps, piece, padded)
    conv_other = flip(conv_same, 1)
    in_full, out_full = unblock((rep & 1).reshape(1), conv_same, conv_other, width)
    return (
        mixed,
        input_grad,
        owned[0],
        in_full,
        owned[2:].T,
        out_full,
        owned[1],
        gate_full,
        up_full,
        down_full,
    )


def solution(mesh):
    placed = (
        P(("rep", "grp"), None),
        P("grp"),
        P("grp", None),
        P("grp", None),
        P("grp", None),
        P("grp"),
        P("grp", None),
        P("grp", None),
        P("grp", None),
        P(("rep", "grp"), None),
    )
    return jax.shard_map(
        shards,
        mesh=mesh,
        in_specs=placed,
        out_specs=(
            P(("rep", "grp"), None),
            P(("rep", "grp"), None),
            P("grp"),
            P("grp", None),
            P("grp", None),
            P("grp", None),
            P("grp"),
            P("grp", None),
            P("grp", None),
            P("grp", None),
        ),
        check_vma=False,
    )
```

```python
import functools

import jax
import jax.numpy as jnp
from jax import lax
from jax.experimental import pallas as pl
from jax.experimental.pallas import tpu as pltpu
from jax.sharding import PartitionSpec as P

EPS = 1e-05
F32, BF16 = jnp.float32, jnp.bfloat16
LIGHT = pl.CostEstimate(flops=1, bytes_accessed=1, transcendentals=0)


def after(value, *others):
    return lax.optimization_barrier((value,) + others)[0]


def from_behind(value, axis, steps):
    count = lax.axis_size(axis)
    first, last = (max(0, -steps), min(count, count - steps))
    return lax.ppermute(value, axis, [(source, source + steps) for source in range(first, last)])


def product(left, right):
    return jnp.dot(left, right, preferred_element_type=F32)


def left_product(left, right):
    return lax.dot_general(left, right, (((0,), (0,)), ((), ())), preferred_element_type=F32)


def right_transposed(left, right):
    return lax.dot_general(left, right, (((1,), (1,)), ((), ())), preferred_element_type=F32)


def turn(value, places):
    count = lax.axis_size("grp")
    return lax.ppermute(value, "grp", [(i, (i + places) % count) for i in range(count)])


def behind(places):
    count = lax.axis_size("grp")
    return lax.rem(lax.axis_index("grp") - places + count, count)


def placed(values):
    out = jnp.zeros((len(values),) + values[0].shape, values[0].dtype)
    for places, value in enumerate(values):
        out = lax.dynamic_update_index_in_dim(out, value, behind(places), 0)
    return out


def sends(parts):
    return [
        lax.dynamic_index_in_dim(parts, behind(-places), 0, keepdims=False)
        for places in range(lax.axis_size("grp"))
    ]


def turned(parts):
    return parts[:1] + [turn(part, places + 1) for places, part in enumerate(parts[1:])]


def total(parts):
    return sum(part.astype(F32) for part in parts)


def flip(value, bit):
    return lax.ppermute(value, "rep", [(i, i ^ bit) for i in range(lax.axis_size("rep"))])


def pair(mine, other, bit, axis):
    low = (lax.axis_index("rep") & bit) == 0
    return jnp.stack([jnp.where(low, mine, other), jnp.where(low, other, mine)], axis)


def same_core():
    chips = lax.axis_size("rep") // 2
    return [[2 * chip + core for chip in range(chips)] for core in range(2)]


def chips_gather(value):
    return lax.all_gather(value, "rep", axis=0, axis_index_groups=same_core())


def chips_gather_two(one, two):
    if lax.axis_size("rep") != 8:
        return chips_gather(one), chips_gather(two)
    one_x, two_y = flip(one, 2), flip(two, 4)
    one, two = pair(one, one_x, 2, 0), pair(two, two_y, 4, 0)
    one_y, two_x = flip(one, 4), flip(two, 2)
    one, two = pair(one, one_y, 4, 0), pair(two, two_x, 2, 1)
    return one.reshape((4,) + one.shape[2:]), two.reshape((4,) + two.shape[2:])


def chips_gather_steps(value):
    half = value.shape[-1] // 2
    return jnp.concatenate(chips_gather_two(value[..., :half], value[..., half:]), axis=-1)


def chips_scatter(value):
    return lax.psum_scatter(
        value, "rep", scatter_dimension=0, tiled=True, axis_index_groups=same_core()
    )


def chips_scatter_steps(value):
    if lax.axis_size("rep") != 8:
        return chips_scatter(value).astype(F32)
    rep = lax.axis_index("rep")
    rows, half = value.shape[0] // 4, value.shape[1] // 2

    def split(part, bit, axis):
        mine = jnp.where((rep & bit) == 0, 0, 1)
        pick = lambda i: lax.dynamic_index_in_dim(part, i, axis, keepdims=False)
        return pick(mine).astype(F32), pick(1 - mine).astype(BF16)

    value = value.reshape(2, 2, rows, 2 * half)
    one, send_one = split(value[..., :half], 2, 1)
    two, send_two = split(value[..., half:], 4, 0)
    one, two = one + flip(send_one, 2).astype(F32), two + flip(send_two, 4).astype(F32)
    one, send_one = split(one, 4, 0)
    two, send_two = split(two, 2, 0)
    one, two = one + flip(send_one, 4).astype(F32), two + flip(send_two, 2).astype(F32)
    return jnp.concatenate([one, two], axis=-1)


def rep_scatter(value):
    return lax.psum_scatter(value, "rep", scatter_dimension=0, tiled=True)


def rep_gather(value):
    return lax.all_gather(value, "rep", axis=0)


def spread_kernel(piece, padded, groups, pair_ref, gate_ref, up_ref):
    reps, _, lanes = pair_ref.shape
    for start, out_ref in ((0, gate_ref), (lanes // 2, up_ref)):
        for j in range(groups):
            for rep in range(reps):
                place, source = (j * reps + rep) * piece, start + j * padded
                out_ref[:, place : place + piece] = pair_ref[
                    rep, :, source : source + piece
                ].astype(F32)


def spread(part, groups, piece, padded):
    reps, rows, lanes = part.shape
    hidden = reps * groups * piece
    tile = 64
    return pl.pallas_call(
        functools.partial(spread_kernel, piece, padded, groups),
        grid=(rows // tile,),
        in_specs=[pl.BlockSpec((reps, tile, lanes), lambda i: (0, i, 0))],
        out_specs=[pl.BlockSpec((tile, hidden), lambda i: (i, 0))] * 2,
        out_shape=[jax.ShapeDtypeStruct((rows, hidden), F32)] * 2,
        compiler_params=pltpu.CompilerParams(vmem_limit_bytes=60 * 2**20),
        cost_estimate=pl.CostEstimate(flops=0, bytes_accessed=rows * hidden * 12, transcendentals=0),
    )(part)


def place_kernel(count, steps, table_ref, *refs):
    del table_ref
    step = pl.program_id(0)
    left_ref, right_ref = refs[-2:]
    for k in range(count):

        @pl.when((step >= k * steps) & (step < (k + 1) * steps))
        def _(k=k):
            left_ref[...] = refs[2 * k][0, 0]
            right_ref[...] = refs[2 * k + 1][0, 0]


def place_weights(left, right, pieces, cores, near, rep, grp):
    _, turns, cut, cols = pieces[0].shape
    own = left.shape[0] // (turns + 1)
    x, y = (rep >> 1) & 1, rep >> 2
    if not near:
        x, y = 1 - x, 1 - y
    rows = lambda places, chip, core: behind(places) * (own // cut) + 2 * chip + core
    table = jnp.stack(
        [
            rows(places, chip, core)
            for which in range(2)
            for core in cores
            for line in range(2)
            for places in range(1, turns + 1)
            for chip in ((2 * y + line, 2 * line + x)[which],)
        ]
    )
    count, steps = len(cores), 2 * turns

    def came(k):
        def index(i, table):
            step = jnp.clip(i - k * steps, 0, steps - 1)
            return (step // turns, step % turns, 0, 0)

        return pl.BlockSpec((1, 1, cut, cols), index)

    anywhere = pl.BlockSpec(memory_space=pl.ANY)
    total_steps = count * steps
    return pl.pallas_call(
        lambda table_ref, *refs: place_kernel(count, steps, table_ref, *refs[2:]),
        grid_spec=pltpu.PrefetchScalarGridSpec(
            num_scalar_prefetch=1,
            grid=(total_steps,),
            in_specs=[anywhere] * 2 + [came(k // 2) for k in range(2 * count)],
            out_specs=[
                pl.BlockSpec((cut, cols), lambda i, table: (table[i], 0)),
                pl.BlockSpec((cut, cols), lambda i, table: (table[total_steps + i], 0)),
            ],
        ),
        out_shape=[jax.ShapeDtypeStruct(left.shape, BF16)] * 2,
        input_output_aliases={1: 0, 2: 1},
        compiler_params=pltpu.CompilerParams(vmem_limit_bytes=60 * 2**20),
        cost_estimate=LIGHT,
    )(table, left, right, *pieces)


def in_kernel(tokens_ref, gain_ref, b_ref, c_ref, x_ref, h_ref, scale_ref, b_out, c_out, x_out, edge_ref):
    @pl.when(pl.program_id(0) == 0)
    def _():
        inputs = tokens_ref[...].astype(F32)
        scale = lax.rsqrt(jnp.mean(inputs * inputs, axis=-1, keepdims=True) + EPS)
        scale_ref[...] = scale
        h_ref[...] = (inputs * scale * gain_ref[...]).astype(BF16)

    h_low = h_ref[...]
    b_part = product(h_low, b_ref[...])
    x_part = product(h_low, x_ref[...])
    b_out[...] = b_part
    x_out[...] = x_part
    c_out[...] = product(h_low, c_ref[...])
    edge_ref[...] = (b_part * x_part)[-edge_ref.shape[0] :]


def in_forward(tokens, gain, left, right):
    rows, width = tokens.shape
    cols = 256
    count = width // cols
    whole = pl.BlockSpec((rows, width), lambda i: (0, 0))
    column = pl.BlockSpec((rows, cols), lambda i: (0, i))
    weight = lambda start: pl.BlockSpec((width, cols), lambda i: (0, start + i))
    part = jax.ShapeDtypeStruct((rows, width), F32)
    return pl.pallas_call(
        in_kernel,
        grid=(count,),
        in_specs=[
            whole,
            pl.BlockSpec((1, width), lambda i: (0, 0)),
            weight(0),
            weight(count),
            weight(0),
        ],
        out_specs=[
            whole,
            pl.BlockSpec((rows, 1), lambda i: (0, 0)),
            column,
            column,
            column,
            pl.BlockSpec((8, cols), lambda i: (0, i)),
        ],
        out_shape=[
            jax.ShapeDtypeStruct((rows, width), BF16),
            jax.ShapeDtypeStruct((rows, 1), F32),
            part,
            part,
            part,
            jax.ShapeDtypeStruct((8, width), F32),
        ],
        compiler_params=pltpu.CompilerParams(vmem_limit_bytes=60 * 2**20),
        cost_estimate=LIGHT,
    )(tokens, gain, left, left, right)


def out_kernel(
    tokens_ref, gain_ref, taps_ref, earlier_ref, b_ref, c_ref, x_ref, w_ref,
    gated_ref, conv_ref, z_ref, resid_ref, normed_ref, scale_ref, h2_ref, sum_ref,
):
    step = pl.program_id(0)
    rows = b_ref.shape[0]
    gated = b_ref[...] * x_ref[...]
    gated_ref[...] = gated
    padded = jnp.concatenate([earlier_ref[...], gated], axis=0)
    conv = taps_ref[0:1] * padded[0:rows]
    for tap in range(1, taps_ref.shape[0]):
        conv = conv + taps_ref[tap : tap + 1] * padded[tap : tap + rows]
    conv_ref[...] = conv
    z_low = (c_ref[...] * conv).astype(BF16)
    z_ref[...] = z_low

    @pl.when(step == 0)
    def _():
        sum_ref[...] = tokens_ref[...].astype(F32)

    sum_ref[...] += product(z_low, w_ref[...])

    @pl.when(step == pl.num_programs(0) - 1)
    def _():
        resid = sum_ref[...]
        resid_ref[...] = resid
        scale = lax.rsqrt(jnp.mean(resid * resid, axis=-1, keepdims=True) + EPS)
        scale_ref[...] = scale
        normed = resid * scale
        normed_ref[...] = normed
        h2_ref[...] = (normed * gain_ref[...]).astype(BF16)


def out_forward(tokens, gain, taps_f, earlier, b_part, c_part, x_part, right):
    rows, width = tokens.shape
    cols = 256
    whole = pl.BlockSpec((rows, width), lambda i: (0, 0))
    column = lambda n: pl.BlockSpec((n, cols), lambda i: (0, i))
    full = lambda kind: jax.ShapeDtypeStruct((rows, width), kind)
    return pl.pallas_call(
        out_kernel,
        grid=(width // cols,),
        in_specs=[
            whole,
            pl.BlockSpec((1, width), lambda i: (0, 0)),
            column(taps_f.shape[0]),
            column(earlier.shape[0]),
            column(rows),
            column(rows),
            column(rows),
            pl.BlockSpec((cols, width), lambda i: (i, 1)),
        ],
        out_specs=[
            column(rows),
            column(rows),
            column(rows),
            whole,
            whole,
            pl.BlockSpec((rows, 1), lambda i: (0, 0)),
            whole,
        ],
        out_shape=[
            full(F32),
            full(F32),
            full(BF16),
            full(F32),
            full(F32),
            jax.ShapeDtypeStruct((rows, 1), F32),
            full(BF16),
        ],
        scratch_shapes=[pltpu.VMEM((rows, width), F32)],
        compiler_params=pltpu.CompilerParams(vmem_limit_bytes=60 * 2**20),
        cost_estimate=LIGHT,
    )(tokens, gain, taps_f, earlier, b_part, c_part, x_part, right)


def mid_kernel(
    second0_ref, second1_ref, up_ref, normed_ref, scale_ref, gain_ref, w_ref, conv_ref, c_ref,
    resid_ref, branch_ref, d_c_ref, d_conv_ref, sum_ref,
):
    step, half_steps = pl.program_id(0), pl.num_programs(0) // 2

    @pl.when(step == 0)
    def _():
        sum_ref[...] = jnp.zeros_like(sum_ref)

    d_second = jnp.where(step < half_steps, second0_ref[...], second1_ref[...]).astype(F32)
    normed = normed_ref[...]
    both = d_second * normed
    sum_ref[...] += jnp.sum(both, axis=0, keepdims=True)
    d_normed = d_second * gain_ref[...]
    mean = jnp.mean(d_normed * normed, axis=-1, keepdims=True)
    d_resid = up_ref[...].astype(F32) + scale_ref[...] * (d_normed - normed * mean)
    resid_ref[...] = d_resid
    branch = d_resid.astype(BF16)
    branch_ref[...] = branch
    d_z = right_transposed(branch, w_ref[...])
    d_c_ref[...] = (d_z * conv_ref[...]).astype(BF16)
    d_conv_ref[...] = d_z * c_ref[...]


def mid_backward(second0, second1, upstream, normed, scale, gain, right, conv, c_part):
    rows, width = normed.shape
    tile = rows // 2
    steps = 2
    row = pl.BlockSpec((tile, width), lambda i: (i, 0))
    first = pl.BlockSpec((tile, width), lambda i: (jnp.minimum(i, steps // 2 - 1), 0))
    last = pl.BlockSpec((tile, width), lambda i: (jnp.maximum(i - steps // 2, 0), 0))
    line = pl.BlockSpec((1, width), lambda i: (0, 0))
    return pl.pallas_call(
        mid_kernel,
        grid=(steps,),
        in_specs=[
            first,
            last,
            row,
            row,
            pl.BlockSpec((tile, 1), lambda i: (i, 0)),
            line,
            pl.BlockSpec((width, width), lambda i: (0, 1)),
            row,
            row,
        ],
        out_specs=[row, row, row, row, line],
        out_shape=[
            jax.ShapeDtypeStruct((rows, width), F32),
            jax.ShapeDtypeStruct((rows, width), BF16),
            jax.ShapeDtypeStruct((rows, width), BF16),
            jax.ShapeDtypeStruct((rows, width), F32),
            jax.ShapeDtypeStruct((1, width), F32),
        ],
        compiler_params=pltpu.CompilerParams(vmem_limit_bytes=60 * 2**20),
        cost_estimate=LIGHT,
    )(second0, second1, upstream, normed, scale, gain, right, conv, c_part)


def taps_kernel(d_conv_ref, later_ref, taps_ref, b_ref, x_ref, u_ref, earlier_ref, d_c_ref, branch_ref, all_ref, sum_ref):
    rows = d_conv_ref.shape[0]
    taps = taps_ref.shape[0]
    d_conv = d_conv_ref[...]
    after_it = jnp.concatenate([d_conv, later_ref[...]], axis=0)
    before_it = jnp.concatenate([earlier_ref[...], u_ref[...]], axis=0)
    d_gated = jnp.zeros_like(d_conv)
    for tap in range(taps):
        ahead = taps - 1 - tap
        d_gated = d_gated + taps_ref[tap : tap + 1] * after_it[ahead : ahead + rows]
        sum_ref[tap : tap + 1] = jnp.sum(d_conv * before_it[tap : tap + rows], axis=0, keepdims=True)
    all_ref[0, 0] = (d_gated * x_ref[...]).astype(BF16)
    all_ref[1, 0] = d_c_ref[...]
    all_ref[2, 0] = (d_gated * b_ref[...]).astype(BF16)
    all_ref[3, 0] = branch_ref[...]


def taps_backward(d_conv, later, taps_f, b_part, x_part, gated, earlier, d_c, branch, block):
    rows, width = d_conv.shape
    taps = taps_f.shape[0]
    cols = 256
    per = block // cols
    column = lambda n: pl.BlockSpec((n, cols), lambda i: (0, i))
    d_all, sums = pl.pallas_call(
        taps_kernel,
        grid=(width // cols,),
        in_specs=[
            column(rows),
            column(taps - 1),
            column(taps),
            column(rows),
            column(rows),
            column(rows),
            column(taps - 1),
            column(rows),
            column(rows),
        ],
        out_specs=[
            pl.BlockSpec((4, 1, rows, cols), lambda i: (0, i // per, 0, i % per)),
            column(taps),
        ],
        out_shape=[
            jax.ShapeDtypeStruct((4, width // block, rows, block), BF16),
            jax.ShapeDtypeStruct((taps, width), F32),
        ],
        compiler_params=pltpu.CompilerParams(vmem_limit_bytes=60 * 2**20),
        cost_estimate=LIGHT,
    )(d_conv, later, taps_f, b_part, x_part, gated, earlier, d_c, branch)
    return d_all.reshape(-1, rows, block), sums


def ffn_kernel(core_ref, same_ref, other_ref, up_same_ref, up_other_ref, pair_ref, down_ref, *refs):
    del core_ref
    act_ref, both_ref, second_ref, mixed_ref = refs[-4:]
    lanes, width = down_ref.shape
    first_half = pl.program_id(0) < pl.num_programs(0) // 2
    rows = lambda ref: ref[...].reshape(-1, width)
    h2 = jnp.where(first_half, rows(same_ref), rows(other_ref))
    up_g = jnp.where(first_half, rows(up_same_ref), rows(up_other_ref))
    both = product(h2, pair_ref[...])
    gate, upper = both[:, :lanes], both[:, lanes:]
    sigma = jax.nn.sigmoid(gate)
    swish = gate * sigma
    act = (swish * upper).astype(BF16)
    act_ref[...] = act
    d_act = right_transposed(up_g, down_ref[...])
    d_gate = (d_act * upper * sigma * (1.0 + gate * (1.0 - sigma))).astype(BF16)
    d_upper = (d_act * swish).astype(BF16)
    both_ref[...] = jnp.concatenate([d_gate, d_upper], axis=1).reshape(both_ref.shape)
    second = right_transposed(both_ref[...].reshape(-1, 2 * lanes), pair_ref[...]).astype(BF16)
    second_ref[...] = second.reshape(second_ref.shape)
    mixed_ref[...] = product(act, down_ref[...]).astype(BF16).reshape(mixed_ref.shape)


def ffn(h2s, ups, w_pair, w_down, core, which, filled=()):
    chips, tile, width = ups[0].shape
    tile //= 2
    lanes = w_down.shape[0]
    natural = len(h2s) == 1
    per = 2
    steps = chips // per
    turns = [lambda i: jnp.minimum(i, steps - 1), lambda i: jnp.maximum(i - steps, 0)]
    side = lambda i, core: jnp.where(i < steps, core[0], 1 - core[0])
    plain = lambda n: pl.BlockSpec((per * tile, n), lambda i, core: (i, 0))
    ordered = lambda n: pl.BlockSpec(
        (per, 1, tile, n), lambda i, core: (i % steps, side(i, core), 0, 0)
    )
    full = lambda w: pl.BlockSpec(w.shape, lambda i, core: (0, 0), pipeline_mode=pl.Buffered(1))
    if natural:
        h2s = [h2s[0].reshape(chips, 2, tile, width)] * 2
        h2_specs = [
            pl.BlockSpec((per, 1, tile, width), lambda i, core, k=k: (turns[k](i), core[0] ^ k, 0, 0))
            for k in range(2)
        ]
    else:
        h2s = [value.reshape(chips, tile, width) for value in h2s]
        h2_specs = [
            pl.BlockSpec((per, tile, width), lambda i, core, k=k: (turns[k](i), 0, 0))
            for k in range(2)
        ]
    tokens = 2 * chips * tile
    placed_ = lambda n: jax.ShapeDtypeStruct((chips, 2, tile, n), BF16)
    acts, boths, second, mixed = pl.pallas_call(
        ffn_kernel,
        grid_spec=pltpu.PrefetchScalarGridSpec(
            num_scalar_prefetch=1,
            grid=(2 * steps,),
            in_specs=h2_specs
            + [
                pl.BlockSpec((per, tile, width), lambda i, core, at=at: (at(i), which, 0))
                for at in turns
            ]
            + [full(w_pair), full(w_down)]
            + [pl.BlockSpec(memory_space=pl.ANY) for _ in filled],
            out_specs=[
                plain(lanes),
                ordered(2 * lanes) if natural else plain(2 * lanes),
                ordered(width),
                pl.BlockSpec(
                    (per, 1, 1, tile, width),
                    lambda i, core: (i % steps, side(i, core), which, 0, 0),
                ),
            ],
        ),
        out_shape=[
            jax.ShapeDtypeStruct((tokens, lanes), BF16),
            placed_(2 * lanes) if natural else jax.ShapeDtypeStruct((tokens, 2 * lanes), BF16),
            placed_(width),
            jax.ShapeDtypeStruct((chips, 2, 2, tile, width), BF16),
        ],
        input_output_aliases={7: 3} if filled else {},
        compiler_params=pltpu.CompilerParams(vmem_limit_bytes=60 * 2**20),
        cost_estimate=pl.CostEstimate(
            flops=17 * tokens * width * lanes, bytes_accessed=0, transcendentals=0
        ),
    )(core, *h2s, *ups, w_pair, w_down, *filled)
    return acts, boths.reshape(tokens, -1), second.reshape(tokens, width), mixed


def grad_kernel(parts, lefts_count, *refs):
    lefts, rights, out_ref, total_ref = (
        refs[:lefts_count],
        refs[lefts_count:-2],
        refs[-2],
        refs[-1],
    )
    step = pl.program_id(0)

    @pl.when(step == 0)
    def _():
        total_ref[...] = jnp.zeros_like(total_ref)

    for start, stop, left, right in parts:

        @pl.when((step >= start) & (step < stop))
        def _(left=left, right=right):
            value = rights[right][...]
            value = value.reshape(-1, value.shape[-1])
            total_ref[...] += left_product(lefts[left][...], value)

    @pl.when(step == pl.num_programs(0) - 1)
    def _():
        out_ref[...] = total_ref[...].astype(BF16)


def grad(lefts, rights, halves=None):
    tile = 480
    n, m = lefts[0].shape[1], rights[0].shape[-1]

    def cuts(arrays):
        out = [0]
        for array in arrays:
            out.append(out[-1] + array.size // array.shape[-1] // tile // (array.ndim - 1))
        return out

    left_cuts, right_cuts = cuts(lefts), cuts(rights)
    edges = sorted(set(left_cuts + right_cuts))
    find = lambda which, step: max(k for k in range(len(which) - 1) if which[k] <= step)
    parts = [
        (start, stop, find(left_cuts, start), find(right_cuts, start))
        for start, stop in zip(edges, edges[1:])
    ]

    def spec(which, k, array):
        at = lambda i: jnp.clip(i, which[k], which[k + 1] - 1) - which[k]
        if array.ndim == 2:
            return pl.BlockSpec((tile, array.shape[1]), lambda i: (at(i), 0))
        half = array.shape[1] // 2
        return pl.BlockSpec((tile // half, half, array.shape[2]), lambda i: (at(i), halves[k], 0))

    return pl.pallas_call(
        functools.partial(grad_kernel, parts, len(lefts)),
        grid=(edges[-1],),
        in_specs=[spec(left_cuts, k, array) for k, array in enumerate(lefts)]
        + [spec(right_cuts, k, array) for k, array in enumerate(rights)],
        out_specs=pl.BlockSpec((n, m), lambda i: (0, 0)),
        out_shape=jax.ShapeDtypeStruct((n, m), BF16),
        scratch_shapes=[pltpu.VMEM((n, m), F32)],
        compiler_params=pltpu.CompilerParams(vmem_limit_bytes=60 * 2**20),
        cost_estimate=pl.CostEstimate(flops=3 * tile * edges[-1] * n * m, bytes_accessed=0, transcendentals=0),
    )(*lefts, *rights)


def block_kernel(count, kept, places_ref, *refs):
    del places_ref
    lefts, rights, refs = refs[:count], refs[count : 2 * count], refs[2 * count :]
    for k in range(count):
        total_ = left_product(lefts[k][0], rights[k][0])
        if not kept:
            refs[k][...] = total_.astype(BF16)
            continue
        total_ = total_ + refs[k][...].astype(F32)
        for which in range(2):

            @pl.when(pl.program_id(0) == which)
            def _(k=k, which=which, total_=total_):
                ref = refs[count + 2 * k + which]
                ref[...] = total_.astype(ref.dtype)


def block_grads(places, lefts, rights, came=(), kept=()):
    count = places.shape[0]
    rows, width = lefts.shape[1:]
    blocks, _, block = rights.shape
    branch = blocks - blocks // 4
    left = lambda k: pl.BlockSpec(
        (1, rows, width // 2), lambda i, places: ((places[k] >= branch).astype(jnp.int32), 0, i)
    )
    right = lambda k: pl.BlockSpec((1, rows, block), lambda i, places: (places[k], 0, 0))
    moving = pl.BlockSpec((width // 2, block), lambda i, places: (i, 0))
    fixed = pl.BlockSpec((width // 2, block), lambda i, places: (0, 0))
    if kept:
        outs = [jax.ShapeDtypeStruct((width // 2, block), kind) for kind in kept]
    else:
        outs = [jax.ShapeDtypeStruct((width, block), BF16)] * count
    return pl.pallas_call(
        functools.partial(block_kernel, count, bool(kept)),
        grid_spec=pltpu.PrefetchScalarGridSpec(
            num_scalar_prefetch=1,
            grid=(2,),
            in_specs=[left(k) for k in range(count)]
            + [right(k) for k in range(count)]
            + [moving for _ in came],
            out_specs=[fixed if kept else moving for _ in outs],
        ),
        out_shape=outs,
        compiler_params=pltpu.CompilerParams(vmem_limit_bytes=40 * 2**20),
        cost_estimate=LIGHT,
    )(places, *([lefts] * count), *([rights] * count), *came)


def unblock_kernel(core_ref, same_ref, other_ref, in_ref, out_ref):
    chips, _, block = same_ref.shape
    first = core_ref[0] == 0
    for chip in range(chips):
        same, other = same_ref[chip].astype(F32), other_ref[chip].astype(F32)
        for core, value in enumerate((jnp.where(first, same, other), jnp.where(first, other, same))):
            place = (2 * chip + core) * block
            if place < in_ref.shape[1]:
                in_ref[:, place : place + block] = value
            else:
                place -= in_ref.shape[1]
                out_ref[:, place : place + block] = value


def unblock(core, same, other, width):
    chips, rows, block = same.shape
    tile = 96
    spec = pl.BlockSpec((chips, tile, block), lambda i, core: (0, i, 0))
    return pl.pallas_call(
        unblock_kernel,
        grid_spec=pltpu.PrefetchScalarGridSpec(
            num_scalar_prefetch=1,
            grid=(rows // tile,),
            in_specs=[spec, spec],
            out_specs=[pl.BlockSpec((tile, n), lambda i, core: (i, 0)) for n in (3 * width, width)],
        ),
        out_shape=[jax.ShapeDtypeStruct((rows, n), F32) for n in (3 * width, width)],
        compiler_params=pltpu.CompilerParams(vmem_limit_bytes=60 * 2**20),
        cost_estimate=pl.CostEstimate(flops=0, bytes_accessed=24 * rows * width, transcendentals=0),
    )(core, same, other)


def shards(
    tokens,
    norm_in,
    in_weight,
    conv_weight,
    out_weight,
    norm_mid,
    gate_weight,
    up_weight,
    down_weight,
    cotangent,
):
    reps, grps = lax.axis_size("rep"), lax.axis_size("grp")
    rep, grp = lax.axis_index("rep"), lax.axis_index("grp")
    chips = reps // 2
    low_core = (rep & 1) == 0
    rows, width = tokens.shape
    taps = conv_weight.shape[1]
    own = in_weight.shape[0]
    hidden = gate_weight.shape[1]
    piece = hidden // (reps * grps)
    padded = -(-piece // 16) * 16
    units = padded * grps
    lanes = -(-units // 128) * 128
    half = rows // 2

    def columns(weight):
        gap, parts = jnp.zeros((own, padded - piece), BF16), []
        for j in range(grps):
            place = j * (hidden // grps) + rep * piece
            parts += [lax.dynamic_slice(weight, (0, place), (own, piece)), gap]
        return jnp.concatenate(parts + [jnp.zeros((own, lanes - units), BF16)], axis=1)

    pair_piece = jnp.concatenate([columns(gate_weight), columns(up_weight)], axis=1)
    down_piece = lax.dynamic_slice_in_dim(down_weight, rep * piece, piece, 0)
    down_piece = jnp.pad(down_piece, ((0, padded - piece), (0, 0)))
    cut = own // reps
    gains = jnp.concatenate([norm_in[None], norm_mid[None], conv_weight.T], axis=0)
    sent = jnp.concatenate(
        [
            lax.dynamic_slice_in_dim(in_weight, rep * cut, cut, 0),
            lax.dynamic_slice_in_dim(out_weight, rep * cut, cut, 0),
        ],
        axis=1,
    )
    fast = reps == 8 and grps == 4
    if fast:
        def first(value):
            half_cols = value.shape[-1] // 2
            return [value[..., :half_cols], value[..., half_cols:]]

        def swap(values, bits):
            return [flip(value, bit) for value, bit in zip(values, bits)]

        def second(values, came):
            return [pair(values[0], came[0], 2, 0), pair(values[1], came[1], 4, 0)]

        def third(values, came):
            both = [pair(values[0], came[0], 4, 0), pair(values[1], came[1], 2, 1)]
            return jnp.concatenate([value.reshape((4,) + value.shape[2:]) for value in both], axis=-1)

        side = -(-gains.size // (cut * 128)) * 128
        gains = jnp.pad(gains.reshape(-1), (0, cut * side - gains.size)).reshape(cut, side)
        sent = jnp.concatenate([sent, gains], axis=1)
        near, far = [turn(sent, 1), turn(sent, 3)], turn(sent, 2)
        ups = first(cotangent)
        left = jnp.zeros((width, 2 * width), BF16)
        left = lax.dynamic_update_slice(left, in_weight[:, : 2 * width], (grp * own, 0))
        right = jnp.zeros((width, 2 * width), BF16)
        right = lax.dynamic_update_slice(right, in_weight[:, 2 * width :], (grp * own, 0))
        right = lax.dynamic_update_slice(right, out_weight, (grp * own, width))
        came = [after(value, pair_piece, left, right, far, *near) for value in swap(ups, (2, 4))]
        ups = second(ups, came)
        w_pair = lax.all_gather(after(pair_piece, far), "grp", axis=0, tiled=True)
        hops = [after(near[0], *came), far, near[1]]
        small = placed([gains] + [value[:, 4 * width :] for value in hops])
        small = small.reshape(grps, -1)[:, : (2 + taps) * own].reshape(grps, 2 + taps, own)
        turns = first(jnp.stack([value[:, : 4 * width] for value in hops]))
        turns_came = swap(turns, (2, 4))
        pieces = second(turns, turns_came)
        cores = (rep & 1, 1 - (rep & 1))
        came = swap(pieces, (4, 2))
        pieces += [flip(value, 1) for value in pieces]
        left, right = place_weights(left, right, pieces, cores, True, rep, grp)
        pieces = [after(value, left) for value in came]
        ups = [after(value, *pieces) for value in ups]
        up_came = swap(ups, (4, 2))
        pieces += [flip(value, 1) for value in pieces]
        left, right = place_weights(left, right, pieces, cores, False, rep, grp)
        w_down = lax.all_gather(after(down_piece, pair_piece), "grp", axis=0, tiled=True)
    else:
        w_pair = lax.all_gather(pair_piece, "grp", axis=0, tiled=True)
        w_down = lax.all_gather(down_piece, "grp", axis=0, tiled=True)
        whole = lax.all_gather(sent, ("grp", "rep"), axis=0, tiled=True)
        left, right = whole[:, : 2 * width], whole[:, 2 * width :]
        small = lax.all_gather(gains, "grp", axis=0)
        ups_same = chips_gather(cotangent)
    small = small.swapaxes(0, 1).reshape(2 + taps, width).astype(F32)
    gain_one, gain_two, taps_f = small[0], small[1], small[2:]

    h_low, scale_one, b_part, c_part, x_part, edge = in_forward(tokens, gain_one[None], left, right)
    earlier = from_behind(edge[edge.shape[0] - (taps - 1) :], "grp", 1)
    gated, conv, z_low, resid, normed_two, scale_two, h2_low = out_forward(
        tokens,
        gain_two[None],
        taps_f,
        earlier,
        b_part,
        c_part,
        x_part,
        right,
    )
    w_x, w_out = right[:, :width], right[:, width:]

    flat = lambda value: value.reshape(chips * half, width)
    h2_last = h2_low[half:]
    if fast:
        parts = first(h2_low[:half])
        came = swap(parts, (2, 4))
        ups_same = third(ups, [after(value, *parts) for value in up_came])
        parts = second(parts, [after(value, w_pair, ups_same) for value in came])
        came = swap(parts, (4, 2))
        same = flat(third(parts, came))
        h2_last = after(h2_last, *came)
    else:
        same = flat(chips_gather(h2_low[:half]))
    h2_first = [same, flip(after(same, w_down) if fast else same, 1)]
    h2_last = [rep_gather(h2_last).reshape(reps * half, width)]
    if lanes > units:
        w_down = jnp.concatenate([w_down, jnp.zeros((lanes - units, width), BF16)], axis=0)

    ups_all = [ups_same, flip(ups_same, 1)]
    core = (rep & 1).reshape(1)
    acts0, boths0, second0, mixed = ffn(h2_first, ups_all, w_pair, w_down, core, 0)
    h2_last[0] = after(h2_last[0], second0)
    acts1, boths1, second1, mixed = ffn(h2_last, ups_all, w_pair, w_down, core, 1, [mixed])
    second0, second1 = rep_scatter(second0), rep_scatter(second1)
    down_grad = grad([after(acts0, mixed), acts1], ups_all * 2, (0, 0, 1, 1))
    down_sends = sends(down_grad[:units].reshape(grps, padded, width)[:, :piece])
    pair_grad = grad(
        [after(h2_first[0], second0, *down_sends), h2_first[1]] + h2_last, [boths0, boths1]
    )
    mixed = rep_scatter(mixed.reshape(reps * rows, width))
    pair_sends = sends(pair_grad.reshape(grps, own, 2 * lanes))
    if fast:
        down_turns = turned(down_sends)
        down_turns[1] = after(down_turns[1], *pair_sends)
        second1, *down_turns = lax.optimization_barrier((second1, *down_turns))
    else:
        down_own = total(turned(down_sends)).astype(BF16)
        pair_own = total(turned(pair_sends)).astype(BF16)

    block = 4 * width // reps
    split = width // block
    if fast:
        d_resid, d_branch, d_c, d_conv, local_mid = mid_backward(
            second0, second1, cotangent, normed_two, scale_two, gain_two[None], right, conv, c_part
        )
        local_mid = local_mid[0]
        later = from_behind(d_conv[: taps - 1], "grp", -1)
        near = [turn(after(pair_sends[k], later), k) for k in (1, 3)]
        down_turns[0] = after(down_turns[0], d_conv)
        down_own = total(down_turns).astype(BF16)
        gated = after(gated, down_own)
        d_all, local_taps = taps_backward(
            d_conv, later, taps_f, b_part, x_part, gated, earlier, d_c, d_branch, block
        )
        local_taps = list(local_taps)
    else:
        d_second = jnp.concatenate([second0, second1], axis=0).astype(F32)
        local_mid = jnp.sum(d_second * normed_two, axis=0)
        d_normed_two = d_second * gain_two
        d_resid = cotangent.astype(F32) + scale_two * (
            d_normed_two - normed_two * jnp.mean(d_normed_two * normed_two, axis=-1, keepdims=True)
        )
        d_branch = d_resid.astype(BF16)
        d_z = right_transposed(d_branch, w_out)
        d_c = d_z * conv
        d_conv = d_z * c_part
        later = from_behind(d_conv[: taps - 1], "grp", -1)
        padded_back = jnp.concatenate([d_conv, later], axis=0)
        d_gated = taps_f[0] * padded_back[taps - 1 : taps - 1 + rows]
        for tap in range(1, taps):
            ahead = taps - 1 - tap
            d_gated = d_gated + taps_f[tap] * padded_back[ahead : ahead + rows]
        before_it = jnp.concatenate([earlier, gated], axis=0)
        local_taps = [jnp.sum(d_conv * before_it[tap : tap + rows], axis=0) for tap in range(taps)]
        d_all = jnp.concatenate([d_gated * x_part, d_c, d_gated * b_part], axis=1).astype(BF16)
        d_all = jnp.concatenate([d_all, d_branch], axis=1)
        d_all = d_all.reshape(rows, reps, block).swapaxes(0, 1)

    lefts = jnp.stack([h_low, z_low])
    if fast:
        places = lambda *ms: jnp.stack([rep ^ m for m in ms])
        grads_one = block_grads(places(7, 3), lefts, d_all)
        flips_one = [flip(value, 1) for value in grads_one]
        grads_two = block_grads(places(5, 1), lefts, after(d_all, *grads_one))
        flips_two = [flip(value, 1) for value in grads_two]
        d_all = after(d_all, *grads_two)
        up6, low6, up2, low2 = block_grads(
            places(6, 2), lefts, d_all, flips_one, (BF16, BF16, BF16, F32)
        )
        ones = flip(jnp.stack([up6, up2]), 2)
        d_all = after(d_all, up6)
        up4, low4, up0, low0 = block_grads(
            places(4, 0), lefts, d_all, flips_two, (F32, BF16, F32, F32)
        )
        twos = flip(jnp.stack([low6, low4]), 4)
        d_all = after(d_all, up4, down_own)
    else:
        summed = jnp.concatenate(
            [
                left_product(h_low if j < 3 * split else z_low, d_all[j]).astype(BF16)
                for j in range(reps)
            ]
        )
        summed = lax.psum_scatter(summed, "rep", scatter_dimension=0, tiled=True)

    d_left = jnp.concatenate([d_all[j] for j in range(2 * split)], axis=1)
    d_right = jnp.concatenate([d_all[2 * split + j] for j in range(split)], axis=1)
    d_hidden = right_transposed(d_left, left) + right_transposed(d_right, w_x)
    normed = tokens.astype(F32) * scale_one
    local_in = jnp.sum(d_hidden * normed, axis=0)
    d_normed = d_hidden * gain_one
    input_grad = d_resid + scale_one * (
        d_normed - normed * jnp.mean(d_normed * normed, axis=-1, keepdims=True)
    )
    sums = jnp.stack([local_in, local_mid] + local_taps)
    if fast:
        far_gate = turn(after(pair_sends[2][:, :lanes], d_left), 2)
        ones, twos, mixed, near[0], near[1], far_gate, _ = lax.optimization_barrier(
            (ones, twos, mixed, near[0], near[1], far_gate, input_grad)
        )
        one6, one2, two6, two4 = ones[0], ones[1], twos[0], twos[1]
        one4_send = (up4 + one6.astype(F32)).astype(BF16)
        two2_send = (low2 + two6.astype(F32)).astype(BF16)
        one4, two2 = flip(one4_send, 4), flip(two2_send, 2)
        far_up = turn(after(pair_sends[2][:, lanes:], one4_send, two2_send), 2)
        sums = after(sums, one4_send, two2_send)
        sums = sums + flip(sums, 1)
        sums_came = swap([sums] * 3, (2, 4, 6))
        sums = (sums + sums_came[0]) + (sums_came[1] + sums_came[2])
        one4, two2, far_up, sums = lax.optimization_barrier((one4, two2, far_up, sums))
        far = jnp.concatenate([far_gate, far_up], axis=1)
        pair_own = total([pair_sends[0], near[0], far, near[1]]).astype(BF16)
        sums = after(sums, pair_own)
        one0 = up0 + one2.astype(F32) + one4.astype(F32)
        two0 = low0 + two4.astype(F32) + two2.astype(F32)
        summed = jnp.concatenate([one0, two0], axis=0).astype(BF16)
        sums = sums.reshape(2 + taps, grps, own).swapaxes(0, 1)
        high = lax.reduce_precision(sums, 8, 7)
        sums = jnp.stack([high.astype(BF16), (sums - high).astype(BF16)], axis=1)
        sums = sums.reshape(grps, -1, block)
        sum_rows = sums.shape[1]
        sums = jnp.pad(sums, ((0, 0), (0, -sum_rows % 16), (0, 0)))
        conv_sends = sends(jnp.concatenate([summed.reshape(grps, own, block), sums], axis=1))
        conv_near = [turn(conv_sends[k], k) for k in (1, 3)]
        conv_far = turn(conv_sends[2], 2)
        conv_turns = [conv_sends[0], conv_near[0], conv_far, conv_near[1]]
    else:
        sums = lax.psum(sums, "rep").reshape(2 + taps, grps, own).swapaxes(0, 1)
        owned = total(turned(sends(sums)))
        conv_turns = turned(sends(summed.reshape(grps, own, block)))
    down_full = rep_gather(down_own).reshape(-1, width)
    if fast:
        down_full = after(down_full, *conv_near)
    down_full = down_full.astype(F32)
    pair_full = rep_gather(pair_own)
    mixed = mixed.astype(F32)
    if fast:
        mixed = after(mixed, *conv_near)
    mixed = (resid + mixed).astype(BF16)
    if fast:
        conv_turns[1] = after(conv_turns[1], mixed, down_full)
        conv_own = total(conv_turns)
        owned = conv_own[own : own + sum_rows].reshape(2, 2 + taps, own).sum(axis=0)
        parts = first(conv_own[:own].astype(BF16))
        came = swap(parts, (2, 4))
        parts = second(parts, came)
        came = swap(parts, (4, 2))
        gate_full, up_full = spread(pair_full, grps, piece, padded)
        conv_same = third(parts, [after(value, gate_full, up_full) for value in came])
    else:
        conv_same = chips_gather(total(conv_turns).astype(BF16))
        gate_full, up_full = spread(pair_full, grps, piece, padded)
    conv_other = flip(conv_same, 1)
    in_full, out_full = unblock((rep & 1).reshape(1), conv_same, conv_other, width)
    return (
        mixed,
        input_grad,
        owned[0],
        in_full,
        owned[2:].T,
        out_full,
        owned[1],
        gate_full,
        up_full,
        down_full,
    )


def solution(mesh):
    placed = (
        P(("rep", "grp"), None),
        P("grp"),
        P("grp", None),
        P("grp", None),
        P("grp", None),
        P("grp"),
        P("grp", None),
        P("grp", None),
        P("grp", None),
        P(("rep", "grp"), None),
    )
    return jax.shard_map(
        shards,
        mesh=mesh,
        in_specs=placed,
        out_specs=(
            P(("rep", "grp"), None),
            P(("rep", "grp"), None),
            P("grp"),
            P("grp", None),
            P("grp", None),
            P("grp", None),
            P("grp"),
            P("grp", None),
            P("grp", None),
            P("grp", None),
        ),
        check_vma=False,
    )
```
